512 devices in a mesh: segment: 16 (over z), expert: 32 (over y, x, core).
Axes of the slice: x: 4, y: 4, z: 16, core: 2. Of those that a mesh axis runs over, the one named last changes fastest.
Arguments:
- q_heads: bfloat16 [32, 2048, 1024], P('expert', 'segment'), may hold values from -6 to 6
- k_heads: bfloat16 [32, 2048, 1024], P('expert', 'segment'), may hold values from -6 to 6
- values: bfloat16 [32, 2048, 2048], P('expert', 'segment'), may hold values from -6 to 6
- beta: bfloat16 [32, 2048, 16], P('expert', 'segment'), may hold values from 0.049804688 to 0.94921875
- decay: bfloat16 [32, 2048, 16], P('expert', 'segment'), may hold values from -1 to 0
- head_gain: float32 [128], replicated, may hold values from 0.1 to 1.9
- suffix_len: int32 [32], P('expert'), may hold values from 256 to 2048, as said below
- store_states: bfloat16 [128, 16, 128, 128], P('expert', 'segment'), may hold values from -3 to 3
- cache_row: int32 [32], replicated, may hold values from 0 to 127
- write_slot: int32 [32], P('expert'), may hold values from 0 to 3
- expert_ids: int32 [32, 2048, 4], P('expert', 'segment'), may hold values from 0 to 511, all different within a row; in each aligned block of 128 rows (0 to 127, 128 to 255, ..., all dimensions but the last counted through in order) at most 2 rows name the same one
- route_weight: float32 [32, 2048, 4], P('expert', 'segment'), may hold values from 0.1 to 0.5
- w_gate: bfloat16 [512, 2048, 256], P(('segment', 'expert')), may hold values from -0.125 to 0.125
- w_up: bfloat16 [512, 2048, 256], P(('segment', 'expert')), may hold values from -0.125 to 0.125
- w_down: bfloat16 [512, 256, 2048], P(('segment', 'expert')), may hold values from -0.375 to 0.375
Outputs:
- mixed_out: bfloat16 [32, 2048, 2048], P('expert', 'segment')
- store_out: bfloat16 [128, 16, 128, 128], P('expert', 'segment')
The draws below stay inside these ranges and needn't reach their ends.
Inputs may be any that keep to these rules, and one draw needn't show every extreme that they name: `expert_ids`: in the 128 positions of one device (aligned blocks of the request-major order) no expert is named by more than 2 routes, a bound that some block reaches. `suffix_len`: some request has exactly 2048.
All inputs are finite; a program needn't handle non-finite values.
Results may differ from the reference program's by a relative error of at most 0.0054.
Values may be sent and summed in bfloat16 or wider, within the bound.
A program may use at most 64 MiB of HBM per device.

```python
import math
import jax
import jax.numpy as jnp
import numpy as np
from jax import lax

HV = 16
HK = 8
DK = 128
D = 2048
TRAILING_PLACES = 2048
EH = 256
TOP = 4
ROWS_DEV = 4
EXPERTS = 512
QUERY_TOTAL = 32
TOK_DEV = 128
CAP = 2
STORE_ROWS = 128
N_SEGMENT = 16
N_EXPERT = 32
DEVICES = 512


def draw_suffix_len(key, part):
    key = jax.random.fold_in(key, 5)
    first, second = jax.random.split(key)
    lengths = jax.random.randint(first, (QUERY_TOTAL,), TRAILING_PLACES // 8, TRAILING_PLACES + 1)
    longest = jax.random.randint(second, (), 0, QUERY_TOTAL)
    return jnp.where(jnp.arange(QUERY_TOTAL) == longest, TRAILING_PLACES, lengths).astype(jnp.int32)


def draw_decay(key, part):
    key = jax.random.fold_in(key, 9)
    fragment_list = jax.random.split(key, 4)
    slowest = math.log(1.0 / (2.0 * TRAILING_PLACES))
    fastest = math.log(1.0 / 30.0)
    share = jax.random.uniform(fragment_list[0], (QUERY_TOTAL, 1, HV))
    nominal_span = jnp.exp(slowest + share * (fastest - slowest))
    span_jitter = jax.random.uniform(fragment_list[1], (QUERY_TOTAL, TRAILING_PLACES, HV), minval=0.5, maxval=1.5)
    spike_span = jax.random.uniform(fragment_list[2], (QUERY_TOTAL, TRAILING_PLACES, 1)) < 4.0 / TRAILING_PLACES
    objective_scalar = jnp.log(jax.random.uniform(fragment_list[3], (QUERY_TOTAL, TRAILING_PLACES, 1), minval=0.5, maxval=0.8))
    return (-(nominal_span * span_jitter) + jnp.where(spike_span, objective_scalar, 0.0)).astype(jnp.float32).astype(jnp.bfloat16)


def set_ends(entries, rng, smallest, largest):
    dims = entries.shape
    spot = [jax.random.randint(jax.random.fold_in(rng, axis), (), 0, dims[axis]) for axis in range(len(dims))]
    entries = entries.at[tuple(spot)].set(smallest)
    longest = dims.index(max(dims))
    spot[longest] = (spot[longest] + 1) % dims[longest]
    return entries.at[tuple(spot)].set(largest)


def block_scale(key, dims, pieces, smallest, largest):
    level, own = 1.0, jax.random.fold_in(key, 6)
    for dim, shards_of in pieces:
        steps = jnp.exp(jax.random.uniform(jax.random.fold_in(own, dim), (shards_of,), jnp.float32, smallest / len(pieces), largest / len(pieces)))
        level = level * jnp.repeat(steps, dims[dim] // shards_of).reshape([-1 if axis == dim else 1 for axis in range(len(dims))])
    return level


def deal_out(stream_key, own, number, rows, number_of, top, bound, slope):
    ranking = jax.random.permutation(stream_key, number_of)
    packed, usual = load_shares(number_of, rows * top, bound, slope, True), load_shares(number_of, rows * top, bound, slope, False)
    places = jnp.arange(number_of)

    def named(sizes, rotation):
        used = int((sizes > 0).sum())
        fixed = max(1, used // 4)
        passed = fixed + (places - fixed + rotation * (used - fixed)) % max(1, number_of - fixed)
        return jnp.zeros((number_of,), jnp.int32).at[ranking[jnp.where(places < fixed, places, passed)]].set(jnp.asarray(sizes, jnp.int32))

    sizes = jnp.where(number % 4 == 0, named(packed, number // 4), named(usual, number - number // 4 - 1))
    mixed = jax.random.permutation(jax.random.fold_in(own, 3), number_of)
    donor, receiver = mixed[0:number_of // 2 * 2:2], mixed[1:number_of // 2 * 2:2]
    room = jnp.minimum(sizes[donor] - 1, bound - sizes[receiver]) // 2
    room = jnp.where((donor == ranking[0]) | (receiver == ranking[0]) | (sizes[receiver] == 0), 0, jnp.maximum(room, 0))
    passed = jax.random.randint(jax.random.fold_in(own, 4), (number_of // 2,), 0, 1 << 20) % (room + 1)
    sizes = sizes.at[donor].add(-passed).at[receiver].add(passed)
    labels = jnp.searchsorted(jnp.cumsum(sizes), jnp.arange(rows * top), side="right").astype(jnp.int32)
    grid = labels.reshape(top, rows).T
    grid = grid[jax.random.permutation(jax.random.fold_in(own, 1), rows)]
    rotation = jax.random.randint(jax.random.fold_in(own, 2), (rows, 1), 0, top)
    return jnp.take_along_axis(grid, (jnp.arange(top)[None, :] + rotation) % top, axis=1)


def load_shares(number_of, total, most, slope, full):
    portions = [(1 << 20) // math.isqrt(rank ** slope) + 1 for rank in range(1, number_of + 1)]
    largest = most if full else min(most, max(-(-total // number_of), total * portions[0] // sum(portions)))
    least = 1 if total - largest >= number_of - 1 else 0
    holding, spare = [largest] + [least] * (number_of - 1), total - largest - least * (number_of - 1)
    while spare > 0:
        movable = [i for i in range(1, number_of) if holding[i] < largest] or [i for i in range(1, number_of) if holding[i] < most]
        mass, remaining = sum([portions[i] for i in movable]), spare
        for i in movable:
            more = min(most - holding[i], max(1, remaining * portions[i] // mass), spare)
            holding[i] = holding[i] + more
            spare = spare - more
    return np.array(holding)


def centred(own_key, shape, scale, most, pieces=(), held_as=jnp.bfloat16):
    array = jax.random.normal(own_key, shape, jnp.float32) * scale
    if len(pieces) > 0:
        array = block_scale(own_key, shape, pieces, -0.22, 0.18) * array
    return jnp.clip(array, min=-most, max=most).astype(held_as)


def setup_inputs(seed: int = 0) -> dict:
    key_list = jax.random.split(jax.random.key(seed), 16)
    q_heads = centred(key_list[0], (QUERY_TOTAL, TRAILING_PLACES, HK * DK), 1.0, 6.0, ((0, 32), (1, 16)))
    k_heads = centred(key_list[1], (QUERY_TOTAL, TRAILING_PLACES, HK * DK), 1.0, 6.0, ((0, 32), (1, 16)))
    values = centred(key_list[2], (QUERY_TOTAL, TRAILING_PLACES, D), 1.0, 6.0, ((0, 32), (1, 16)))
    beta = jnp.clip(0.049804688 + 0.89941406 * jax.random.uniform(key_list[3], (QUERY_TOTAL, TRAILING_PLACES, HV), jnp.float32) ** block_scale(key_list[3], (QUERY_TOTAL, TRAILING_PLACES, HV), ((0, 32), (1, 16)), -0.2, 0.2), 0.049804688, 0.94921875).astype(jnp.bfloat16)
    decay = draw_decay(jax.random.fold_in(key_list[15], 71), 0)
    head_gain = jnp.clip(1.0 + 0.18 * jax.random.normal(key_list[5], (DK,), jnp.float32), 0.1, 1.9)
    suffix_len = draw_suffix_len(jax.random.fold_in(key_list[15], 71), 0)
    store_states = centred(key_list[7], (STORE_ROWS, HV, DK, DK), 0.5, 3.0, ((0, 32), (1, 16)))
    cache_row = set_ends(jax.random.randint(key_list[8], (QUERY_TOTAL,), 0, STORE_ROWS), jax.random.fold_in(key_list[8], 1), 0, STORE_ROWS - 1).astype(jnp.int32)
    write_slot = set_ends(jax.random.randint(key_list[9], (QUERY_TOTAL,), 0, ROWS_DEV), jax.random.fold_in(key_list[9], 1), 0, ROWS_DEV - 1).astype(jnp.int32)
    expert_ids_keys = jax.random.split(jax.random.fold_in(key_list[10], 1), QUERY_TOTAL * TRAILING_PLACES // TOK_DEV)
    expert_ids_turns = jax.random.permutation(jax.random.fold_in(key_list[10], 3), QUERY_TOTAL * TRAILING_PLACES // TOK_DEV)
    expert_ids = jax.vmap(lambda own, number: deal_out(jax.random.fold_in(key_list[10], 2), own, number, TOK_DEV, EXPERTS, TOP, CAP, 2))(expert_ids_keys, expert_ids_turns).reshape((QUERY_TOTAL, TRAILING_PLACES, TOP))
    route_weight = jnp.clip(0.1 + 0.4 * jax.random.uniform(key_list[11], (QUERY_TOTAL, TRAILING_PLACES, TOP), jnp.float32) ** block_scale(key_list[11], (QUERY_TOTAL, TRAILING_PLACES, TOP), ((0, 32), (1, 16)), -0.2, 0.2), 0.1, 0.5)
    w_gate = centred(key_list[12], (EXPERTS, D, EH), D ** -0.5, 0.125, ((0, 512),))
    w_up = centred(key_list[13], (EXPERTS, D, EH), D ** -0.5, 0.125, ((0, 512),))
    w_down = centred(key_list[14], (EXPERTS, EH, D), EH ** -0.5, 0.375, ((0, 512),))
    return {"q_heads": q_heads, "k_heads": k_heads, "values": values, "beta": beta, "decay": decay, "head_gain": head_gain, "suffix_len": suffix_len, "store_states": store_states, "cache_row": cache_row, "write_slot": write_slot, "expert_ids": expert_ids, "route_weight": route_weight, "w_gate": w_gate, "w_up": w_up, "w_down": w_down}


def unit_heads(block, factor):
    shaped = block.astype(jnp.float32).reshape(QUERY_TOTAL, TRAILING_PLACES, HK, DK)
    shaped = jnp.repeat(shaped, HV // HK, axis=2)
    return shaped * lax.rsqrt(lax.optimization_barrier(jnp.sum(shaped * shaped, axis=-1, keepdims=True)) + 1e-06) * factor

def reference(q_heads, k_heads, values, beta, decay, head_gain, suffix_len, store_states, cache_row, write_slot, expert_ids, route_weight, w_gate, w_up, w_down):
    precise = lax.Precision.HIGHEST
    queries = unit_heads(q_heads, DK ** (-0.5))
    keys_unit = unit_heads(k_heads, 1.0)
    values_f = values.astype(jnp.float32).reshape(QUERY_TOTAL, TRAILING_PLACES, HV, DK)
    valid = (jnp.arange(TRAILING_PLACES, dtype=jnp.int32)[None, :] < suffix_len[:, None]).astype(jnp.float32)
    strength = beta.astype(jnp.float32) * valid[..., None]
    log_decay = decay.astype(jnp.float32) * valid[..., None]
    initial = store_states[cache_row].astype(jnp.float32)

    def advance(state, inputs):
        query, key_now, value, write, logg = inputs
        keep = jnp.exp(logg)[..., None]
        recalled = jnp.einsum('rhi,rhij->rhj', key_now, state, precision=precise)
        update = write[..., None] * (value - keep * recalled)
        state = keep[..., None] * state + jnp.einsum('rhi,rhj->rhij', key_now, update, precision=precise)
        return (state, jnp.einsum('rhi,rhij->rhj', query, state, precision=precise))
    inputs = tuple((jnp.moveaxis(block, 1, 0) for block in (queries, keys_unit, values_f, strength, log_decay)))
    final_state, raw = lax.scan(advance, initial, inputs)
    raw = jnp.moveaxis(raw, 0, 1) * valid[..., None, None]
    normed = raw * lax.rsqrt(lax.optimization_barrier(jnp.mean(raw * raw, axis=-1, keepdims=True)) + 1e-06) * head_gain.astype(jnp.float32)
    mixed = normed.reshape(QUERY_TOTAL, TRAILING_PLACES, D).astype(jnp.bfloat16)
    columns_view = store_states.reshape(N_EXPERT, ROWS_DEV, HV, DK, DK)
    store_out = columns_view.at[jnp.arange(QUERY_TOTAL, dtype=jnp.int32), write_slot].set(final_state.astype(jnp.bfloat16)).reshape(store_states.shape)
    per_device = TOK_DEV * TOP
    ids_dev = expert_ids.reshape(QUERY_TOTAL, N_SEGMENT, TOK_DEV, TOP).transpose(1, 0, 2, 3).reshape(DEVICES, per_device)
    weight_dev = route_weight.reshape(QUERY_TOTAL, N_SEGMENT, TOK_DEV, TOP).transpose(1, 0, 2, 3).reshape(DEVICES, per_device)
    token_index = jnp.arange(N_EXPERT, dtype=jnp.int32)[None, :, None] * TRAILING_PLACES + jnp.arange(N_SEGMENT, dtype=jnp.int32)[:, None, None] * TOK_DEV + jnp.arange(TOK_DEV, dtype=jnp.int32)[None, None, :]
    token_pair = jnp.repeat(token_index.reshape(DEVICES, TOK_DEV), TOP, axis=1)
    order = jnp.arange(per_device, dtype=jnp.int32)

    def rank_of(routes):
        earlier = (routes[:, None] == routes[None, :]) & (order[None, :] < order[:, None])
        return lax.optimization_barrier(jnp.sum(earlier.astype(jnp.int32), axis=1)).astype(jnp.int32)
    ranks = lax.map(rank_of, ids_dev)
    position = jnp.arange(DEVICES, dtype=jnp.int32)[:, None] * CAP + ranks
    table = jnp.full((EXPERTS, DEVICES * CAP), QUERY_TOTAL * TRAILING_PLACES, jnp.int32).at[ids_dev, position].set(token_pair)
    scales = jnp.zeros((EXPERTS, DEVICES * CAP), jnp.float32).at[ids_dev, position].set(weight_dev)
    flat = jnp.concatenate([mixed.reshape(QUERY_TOTAL * TRAILING_PLACES, D), jnp.zeros((1, D), jnp.bfloat16)], axis=0)

    def expert_step(total, inputs):
        gate_w, up_w, down_w, rows_index, row_scale = inputs
        rows = flat[rows_index]
        gate_part = jnp.dot(rows, gate_w, preferred_element_type=jnp.float32)
        up_part = jnp.dot(rows, up_w, preferred_element_type=jnp.float32)
        hidden = (jax.nn.silu(gate_part) * up_part).astype(jnp.bfloat16)
        result = jnp.dot(hidden, down_w, preferred_element_type=jnp.float32).astype(jnp.bfloat16)
        total = total.at[rows_index].add(row_scale[:, None] * result.astype(jnp.float32))
        return (total, None)
    total, unused = lax.scan(expert_step, flat.astype(jnp.float32), (w_gate, w_up, w_down, table, scales))
    mixed_out = total[:-1].astype(jnp.bfloat16).reshape(QUERY_TOTAL, TRAILING_PLACES, D)
    return (mixed_out, store_out)
```

```python
import jax
import jax.numpy as jnp
from jax import lax
from jax.experimental import pallas as pl
from jax.experimental.pallas import tpu as pltpu
from jax.sharding import PartitionSpec as P

BLOCK = 128
MESH = pl.DeviceIdType.MESH


def unit_rows(block, factor):
    squares = jnp.sum(block * block, axis=-1, keepdims=True)
    return block * lax.rsqrt(squares + 1e-06) * factor


def by_blocks(block, nblocks):
    return block.reshape(nblocks, BLOCK, block.shape[1], block.shape[2]).transpose(2, 0, 1, 3)


def unit_lower_inverse(lower_part, precise):
    nilpotent = -lower_part
    identity = jnp.eye(BLOCK, dtype=jnp.float32)
    inverse = identity + nilpotent
    power = nilpotent
    for level in range(BLOCK.bit_length() - 2):
        power = jnp.einsum("hnts,hnsu->hntu", power, power, precision=precise)
        inverse = inverse + jnp.einsum("hnts,hnsu->hntu", inverse, power, precision=precise)
    return inverse


def moe_kernel(
    idx_ref,
    rows_ref,
    base_ref,
    mix_ref,
    gate_ref,
    up_ref,
    down_ref,
    out_ref,
    climb,
    sink,
    pick,
    stage,
    arrive,
    back,
    flat,
    sum_up,
    sum_down,
    got_up,
    got_down,
    tall,
    wide,
    climb_send,
    climb_recv,
    sink_send,
    sink_recv,
    stage_send,
    arrive_recv,
    back_send,
    back_recv,
    up_send,
    up_recv,
    down_send,
    down_recv,
):
    segments = lax.axis_size("segment")
    columns = lax.axis_size("expert")
    pairs = segments // 2
    tok = rows_ref.shape[0]
    heads = rows_ref.shape[1]
    lane = rows_ref.shape[2]
    half = tok // 2
    seg = lax.axis_index("segment")
    col = lax.axis_index("expert")
    above = lax.rem(seg + 1, segments)
    below = lax.rem(seg + segments - 1, segments)

    barrier = pltpu.get_barrier_semaphore()

    def greet(step, carry):
        other = lax.rem(col + step, columns)
        pl.semaphore_signal(barrier, inc=1, device_id=(seg, other), device_id_type=MESH)
        return carry

    lax.fori_loop(1, columns, greet, 0)
    pl.semaphore_signal(barrier, inc=1, device_id=(above, col), device_id_type=MESH)
    pl.semaphore_signal(barrier, inc=1, device_id=(below, col), device_id_type=MESH)
    pl.semaphore_wait(barrier, columns + 1)

    def part(ref, h):
        return ref.at[pl.ds(h * half, half)]

    def climb_copy(source, slot, h):
        return pltpu.make_async_remote_copy(
            src_ref=part(source, h),
            dst_ref=part(climb.at[slot], h),
            send_sem=climb_send.at[slot, h],
            recv_sem=climb_recv.at[slot, h],
            device_id=(above, col),
            device_id_type=MESH,
        )

    def sink_copy(source, slot, h):
        return pltpu.make_async_remote_copy(
            src_ref=part(source, h),
            dst_ref=part(sink.at[slot], h),
            send_sem=sink_send.at[slot, h],
            recv_sem=sink_recv.at[slot, h],
            device_id=(below, col),
            device_id_type=MESH,
        )

    for h in range(2):
        climb_copy(rows_ref, 0, h).start()
        sink_copy(rows_ref, 1, h).start()
    sink[0] = rows_ref[...]

    def rows_to_wide(rows):
        tall[...] = rows.reshape(tok * heads, lane).astype(jnp.float32)
        for j in range(heads):
            wide[:, j * lane : (j + 1) * lane] = tall[pl.ds(j, tok, stride=heads), :].astype(
                jnp.bfloat16
            )

    def send_out(source, target, send_sem, recv_sem, p, i):
        other = lax.rem(col + i, columns)

        @pl.when(i == 0)
        def _():
            pltpu.make_async_copy(source.at[p, col], target.at[p, col], recv_sem.at[p]).start()

        @pl.when(i > 0)
        def _():
            pltpu.make_async_remote_copy(
                src_ref=source.at[p, other],
                dst_ref=target.at[p, col],
                send_sem=send_sem.at[p],
                recv_sem=recv_sem.at[p],
                device_id=(seg, other),
                device_id_type=MESH,
            ).start()

    def wait_all(target, sem, p):
        pltpu.make_async_copy(target.at[p], target.at[p], sem.at[p]).wait()

    def wait_sent(source, sem, p):
        piece = source.at[p, pl.ds(0, columns - 1)]
        pltpu.make_async_copy(piece, piece, sem.at[p]).wait()

    def dispatch(p):
        pick[0] = sink[p]
        pick[1] = climb[p]

        def one(i, carry):
            other = lax.rem(col + i, columns)
            for r in range(4):
                stage[p, other, r] = pick[r // 2, idx_ref[p, other, r]]
            send_out(stage, arrive, stage_send, arrive_recv, p, i)
            return carry

        lax.fori_loop(0, columns, one, 0)

    def experts(p):
        wait_all(arrive, arrive_recv, p)
        wait_sent(stage, stage_send, p)
        rows_to_wide(arrive[p].reshape(tok, heads, lane))
        gate_part = jnp.dot(wide[...], gate_ref[...], preferred_element_type=jnp.float32)
        up_part = jnp.dot(wide[...], up_ref[...], preferred_element_type=jnp.float32)
        hidden = (gate_part * jax.nn.sigmoid(gate_part) * up_part).astype(jnp.bfloat16)
        for j in range(heads):
            tall[pl.ds(j, tok, stride=heads), :] = jnp.dot(
                hidden,
                down_ref[:, j * lane : (j + 1) * lane],
                preferred_element_type=jnp.float32,
            )
        stage[p] = tall[...].astype(jnp.bfloat16).reshape(columns, 4, heads, lane)

        def one(i, carry):
            send_out(stage, back, back_send, back_recv, p, i)
            return carry

        lax.fori_loop(0, columns, one, 0)

    def land(p):
        wait_all(back, back_recv, p)
        rows_to_wide(back[p].reshape(tok, heads, lane))
        flat[p] = wide[...]

    def gather_step(p, carry):
        for h in range(2):
            climb_copy(rows_ref, p, h).wait_recv()

            @pl.when(p < pairs - 1)
            def _():
                climb_copy(climb.at[p], p + 1, h).start()

            @pl.when(p >= 1)
            def _():
                sink_copy(rows_ref, p, h).wait_recv()

                @pl.when(p < pairs - 1)
                def _():
                    sink_copy(sink.at[p], p + 1, h).start()

        dispatch(p)

        @pl.when(p >= 1)
        def _():
            experts(p - 1)

        @pl.when(p >= 2)
        def _():
            land(p - 2)

        return carry

    lax.fori_loop(0, pairs, gather_step, 0)
    experts(pairs - 1)
    land(pairs - 2)
    land(pairs - 1)

    def term(p, source, h):
        weights = mix_ref[p, source, pl.ds(h * half, half), :]
        rows = flat[p]
        slots = rows.shape[0]
        return jnp.dot(
            weights[:, :slots], rows, preferred_element_type=jnp.float32
        ) + jnp.dot(weights[:, slots:], rows, preferred_element_type=jnp.float32)

    def up_copy(i, h):
        return pltpu.make_async_remote_copy(
            src_ref=part(sum_up.at[i], h),
            dst_ref=part(got_up.at[i], h),
            send_sem=up_send.at[i, h],
            recv_sem=up_recv.at[i, h],
            device_id=(above, col),
            device_id_type=MESH,
        )

    def down_copy(i, h):
        return pltpu.make_async_remote_copy(
            src_ref=part(sum_down.at[i], h),
            dst_ref=part(got_down.at[i], h),
            send_sem=down_send.at[i, h],
            recv_sem=down_recv.at[i, h],
            device_id=(below, col),
            device_id_type=MESH,
        )

    for h in range(2):
        spot = pl.ds(h * half, half)
        sum_up[0, spot] = term(pairs - 1, 1, h).astype(jnp.bfloat16)
        up_copy(0, h).start()
        sum_down[0, spot] = term(pairs - 2, 1, h).astype(jnp.bfloat16)
        down_copy(0, h).start()

    def reduce_step(i, carry):
        for h in range(2):
            spot = pl.ds(h * half, half)
            mine = term(pairs - i, 0, h)
            up_copy(i - 1, h).wait_recv()
            sum_up[i, spot] = (mine + got_up[i - 1, spot].astype(jnp.float32)).astype(jnp.bfloat16)
            up_copy(i, h).start()

            @pl.when(i < pairs - 1)
            def _():
                mine = term(pairs - 2 - i, 1, h)
                down_copy(i - 1, h).wait_recv()
                sum_down[i, spot] = (mine + got_down[i - 1, spot].astype(jnp.float32)).astype(
                    jnp.bfloat16
                )
                down_copy(i, h).start()

        return carry

    lax.fori_loop(1, pairs, reduce_step, 0)
    for h in range(2):
        spot = pl.ds(h * half, half)
        total = base_ref[spot, :].astype(jnp.float32) + term(0, 0, h)
        down_copy(pairs - 2, h).wait_recv()
        total = total + got_down[pairs - 2, spot].astype(jnp.float32)
        up_copy(pairs - 1, h).wait_recv()
        total = total + got_up[pairs - 1, spot].astype(jnp.float32)
        out_ref[spot, :] = total.astype(jnp.bfloat16)

    def drain(p, carry):
        wait_sent(stage, back_send, p)
        for h in range(2):
            climb_copy(rows_ref, p, h).wait_send()
            up_copy(p, h).wait_send()

            @pl.when(p >= 1)
            def _():
                sink_copy(rows_ref, p, h).wait_send()
                down_copy(p - 1, h).wait_send()

        return carry

    lax.fori_loop(0, pairs, drain, 0)


def moe(idx, rows, base, mix, w_gate, w_up, w_down):
    segments = lax.axis_size("segment")
    columns = lax.axis_size("expert")
    pairs = segments // 2
    tok, heads, lane = rows.shape
    width = base.shape[1]
    slots = columns * 4
    bf = jnp.bfloat16
    dma = pltpu.SemaphoreType.DMA
    whole = pl.BlockSpec(memory_space=pltpu.VMEM)
    return pl.pallas_call(
        moe_kernel,
        out_shape=jax.ShapeDtypeStruct((tok, width), bf),
        in_specs=[pl.BlockSpec(memory_space=pltpu.SMEM)] + [whole] * 6,
        out_specs=whole,
        scratch_shapes=[
            pltpu.VMEM((pairs, tok, heads, lane), bf),
            pltpu.VMEM((pairs, tok, heads, lane), bf),
            pltpu.VMEM((2, tok, heads, lane), bf),
            pltpu.VMEM((pairs, columns, 4, heads, lane), bf),
            pltpu.VMEM((pairs, columns, 4, heads, lane), bf),
            pltpu.VMEM((pairs, columns, 4, heads, lane), bf),
            pltpu.VMEM((pairs, slots, width), bf),
            pltpu.VMEM((pairs, tok, width), bf),
            pltpu.VMEM((pairs - 1, tok, width), bf),
            pltpu.VMEM((pairs, tok, width), bf),
            pltpu.VMEM((pairs - 1, tok, width), bf),
            pltpu.VMEM((tok * heads, lane), jnp.float32),
            pltpu.VMEM((tok, width), bf),
            dma((pairs, 2)),
            dma((pairs, 2)),
            dma((pairs, 2)),
            dma((pairs, 2)),
            dma((pairs,)),
            dma((pairs,)),
            dma((pairs,)),
            dma((pairs,)),
            dma((pairs, 2)),
            dma((pairs, 2)),
            dma((pairs - 1, 2)),
            dma((pairs - 1, 2)),
        ],
        compiler_params=pltpu.CompilerParams(
            collective_id=1, has_side_effects=True, vmem_limit_bytes=60 * 1024 * 1024
        ),
    )(idx, rows, base, mix, w_gate, w_up, w_down)


def route_tables(expert_ids, route_weight):
    segments = lax.axis_size("segment")
    columns = lax.axis_size("expert")
    seg = lax.axis_index("segment")
    pairs = segments // 2
    tok, top = expert_ids.shape
    routes = jnp.concatenate([expert_ids.T.astype(jnp.float32), route_weight.T], axis=0)
    routes = lax.all_gather(routes, "segment", axis=0, tiled=False)
    step = jnp.arange(pairs, dtype=jnp.int32)
    place = jnp.stack([seg + step, seg + segments - 1 - step], axis=1) % segments
    routes = routes[place]
    here = (seg * columns + jnp.arange(columns, dtype=jnp.int32)).astype(jnp.float32)
    same = routes[:, :, None, :top, :] == here[None, None, :, None, None]
    weight = jnp.sum(jnp.where(same, routes[:, :, None, top:, :], 0.0), axis=3)
    named = jnp.any(same, axis=3)
    token = jnp.arange(tok, dtype=jnp.int32)
    first = jnp.min(jnp.where(named, token, tok), axis=-1)
    last = jnp.max(jnp.where(named, token, -1), axis=-1)
    index = jnp.stack([first % tok, jnp.maximum(last, 0)], axis=-1)
    index = index.transpose(0, 2, 1, 3).reshape(pairs, columns, 4)
    at_first = jnp.where(token == first[..., None], weight, 0.0)
    at_last = jnp.where((token == last[..., None]) & (last != first)[..., None], weight, 0.0)
    both = jnp.stack([at_first, at_last], axis=3)
    none = jnp.zeros_like(both[:, 0])
    mix = jnp.stack(
        [
            jnp.concatenate([both[:, 0], none], axis=2),
            jnp.concatenate([none, both[:, 1]], axis=2),
        ],
        axis=1,
    )
    mix = mix.reshape(pairs, 2, columns * 4, tok).transpose(0, 1, 3, 2)
    high = lax.reduce_precision(mix, 8, 7)
    low = lax.reduce_precision(mix - high, 8, 7)
    mix = jnp.concatenate([high, low], axis=-1).astype(jnp.bfloat16)
    return index, mix


def shards(
    q_heads,
    k_heads,
    values,
    beta,
    decay,
    head_gain,
    suffix_len,
    store_states,
    cache_row,
    write_slot,
    expert_ids,
    route_weight,
    w_gate,
    w_up,
    w_down,
):
    precise = lax.Precision.HIGHEST
    segments = lax.axis_size("segment")
    columns = lax.axis_size("expert")
    column = lax.axis_index("expert")
    tok_dev = q_heads.shape[1]
    heads_here = store_states.shape[1]
    key_dim = store_states.shape[2]
    head_total = values.shape[2] // key_dim
    repeat_count = head_total // (q_heads.shape[2] // key_dim)

    def widen(block):
        shaped = block[0].reshape(tok_dev, -1, key_dim)
        return jnp.repeat(shaped, repeat_count, axis=1).reshape(tok_dev, head_total * key_dim)

    packed = jnp.stack([widen(q_heads), widen(k_heads), values[0]])
    gating = jnp.stack([beta[0], decay[0]])
    packed, gating = (
        lax.all_to_all(packed, "segment", split_axis=2, concat_axis=1, tiled=True),
        lax.all_to_all(gating, "segment", split_axis=2, concat_axis=1, tiled=True),
    )
    suffix = packed.shape[1]
    nblocks = suffix // BLOCK
    my_row = cache_row[column]
    empty_state = jnp.zeros(store_states.shape[1:], jnp.bfloat16)
    piece = lax.all_gather(store_states, "expert", axis=0, tiled=True)
    inside = (my_row >= 0) & (my_row < piece.shape[0])
    taken = lax.dynamic_index_in_dim(
        piece, jnp.clip(my_row, 0, piece.shape[0] - 1), 0, keepdims=False
    )
    initial = jnp.where(inside, taken, empty_state)
    queries = by_blocks(
        unit_rows(
            packed[0].astype(jnp.float32).reshape(suffix, heads_here, key_dim), key_dim ** (-0.5)
        ),
        nblocks,
    )
    keys_unit = by_blocks(
        unit_rows(packed[1].astype(jnp.float32).reshape(suffix, heads_here, key_dim), 1.0), nblocks
    )
    values_f = by_blocks(
        packed[2].astype(jnp.float32).reshape(suffix, heads_here, key_dim), nblocks
    )
    valid = (jnp.arange(suffix, dtype=jnp.int32) < suffix_len[0]).astype(jnp.float32)
    strength = (
        (gating[0].astype(jnp.float32) * valid[:, None])
        .reshape(nblocks, BLOCK, heads_here)
        .transpose(2, 0, 1)
    )
    log_decay = (
        (gating[1].astype(jnp.float32) * valid[:, None])
        .reshape(nblocks, BLOCK, heads_here)
        .transpose(2, 0, 1)
    )
    cumulative = jnp.cumsum(log_decay, axis=-1)
    spread = cumulative[..., :, None] - cumulative[..., None, :]
    strict = jnp.tril(jnp.ones((BLOCK, BLOCK), bool), -1)
    inclusive = jnp.tril(jnp.ones((BLOCK, BLOCK), bool), 0)
    below = jnp.where(strict, jnp.exp(jnp.where(strict, spread, 0.0)), 0.0)
    upto = jnp.where(inclusive, jnp.exp(jnp.where(inclusive, spread, 0.0)), 0.0)
    key_gram = jnp.einsum("hnti,hnsi->hnts", keys_unit, keys_unit, precision=precise)
    lower_part = strength[..., None] * below * key_gram
    growth = jnp.exp(cumulative)
    targets = jnp.concatenate(
        [strength[..., None] * values_f, (strength * growth)[..., None] * keys_unit], axis=-1
    )
    inverse = unit_lower_inverse(lower_part, precise)
    solved = jnp.einsum("hnts,hnsj->hntj", inverse, targets, precision=precise)
    pseudo = solved[..., :key_dim]
    weights_wy = solved[..., key_dim:]
    tail_decay = jnp.exp(cumulative[..., -1:] - cumulative)
    keys_tail = keys_unit * tail_decay[..., None]
    transition = growth[..., -1][..., None, None] * jnp.eye(
        key_dim, dtype=jnp.float32
    ) - jnp.einsum("hnti,hntj->hnij", keys_tail, weights_wy, precision=precise)
    injection = jnp.einsum("hnti,hntj->hnij", keys_tail, pseudo, precision=precise)

    def advance(state, inputs):
        matrix, offset = inputs
        return (jnp.einsum("hij,hjk->hik", matrix, state, precision=precise) + offset, state)

    final_state, starts = lax.scan(
        advance,
        initial.astype(jnp.float32),
        (jnp.moveaxis(transition, 1, 0), jnp.moveaxis(injection, 1, 0)),
    )
    starts = jnp.moveaxis(starts, 0, 1)
    corrected = pseudo - jnp.einsum("hnti,hnij->hntj", weights_wy, starts, precision=precise)
    scores = upto * jnp.einsum("hnti,hnsi->hnts", queries, keys_unit, precision=precise)
    raw = growth[..., None] * jnp.einsum("hnti,hnij->hntj", queries, starts, precision=precise)
    raw = raw + jnp.einsum("hnts,hnsj->hntj", scores, corrected, precision=precise)
    raw = raw * valid.reshape(nblocks, BLOCK)[None, :, :, None]
    normed = raw * lax.rsqrt(jnp.mean(raw * raw, axis=-1, keepdims=True) + 1e-06) * head_gain
    mixed_heads = (
        normed.transpose(1, 2, 0, 3).reshape(suffix, heads_here * key_dim).astype(jnp.bfloat16)
    )
    store_out = lax.dynamic_update_index_in_dim(
        store_states, final_state.astype(jnp.bfloat16), write_slot[0], 0
    )
    mixed = lax.all_to_all(mixed_heads, "segment", split_axis=0, concat_axis=1, tiled=True)
    index, mix = route_tables(expert_ids[0], route_weight[0])
    rows = mixed.reshape(tok_dev, head_total, key_dim)
    out = moe(index, rows, mixed, mix, w_gate[0], w_up[0], w_down[0])
    return (out[None], store_out)


def solution(mesh):
    return jax.shard_map(
        shards,
        mesh=mesh,
        in_specs=(
            P("expert", "segment", None),
            P("expert", "segment", None),
            P("expert", "segment", None),
            P("expert", "segment", None),
            P("expert", "segment", None),
            P(),
            P("expert"),
            P("expert", "segment", None, None),
            P(),
            P("expert"),
            P("expert", "segment", None),
            P("expert", "segment", None),
            P(("segment", "expert"), None, None),
            P(("segment", "expert"), None, None),
            P(("segment", "expert"), None, None),
        ),
        out_specs=(P("expert", "segment", None), P("expert", "segment", None, None)),
        check_vma=False,
    )
```

```python
import jax
import jax.numpy as jnp
from jax import lax
from jax.experimental import pallas as pl
from jax.experimental.pallas import tpu as pltpu
from jax.sharding import PartitionSpec as P

MESH = pl.DeviceIdType.MESH


def halves(block):
    high = block.astype(jnp.bfloat16)
    low = (block - high.astype(jnp.float32)).astype(jnp.bfloat16)
    return high, low


def left_pair(block):
    high, low = halves(block)
    return jnp.concatenate([high, low], axis=1)


def right_pair(block):
    high, low = halves(block)
    row = jnp.concatenate([high, low], axis=1)
    return jnp.concatenate([row, row], axis=0)


def paired_dot(left, right):
    both = jnp.dot(left, right, preferred_element_type=jnp.float32)
    width = both.shape[1] // 2
    return both[:, :width] + both[:, width:]


def unit_rows(block, factor):
    squares = jnp.sum(block * block, axis=-1, keepdims=True)
    return block * (lax.rsqrt(squares + 1e-06) * factor)


def delta_kernel(
    len_ref,
    row_ref,
    q_ref,
    k_ref,
    v_ref,
    beta_ref,
    decay_ref,
    gain_ref,
    store_ref,
    mixed_ref,
    rows_ref,
    final_ref,
    offer,
    taken,
    origin,
    held,
    passed,
    step_left,
    step_add,
    ends,
    tall,
    strength_ref,
    total_ref,
    across_ref,
    offer_send,
    taken_recv,
    origin_send,
    held_recv,
    passed_send,
    ends_send,
    final_recv,
):
    segments = lax.axis_size("segment")
    columns = lax.axis_size("expert")
    seg = lax.axis_index("segment")
    col = lax.axis_index("expert")
    tok = q_ref.shape[0]
    dim = store_ref.shape[-1]
    cached = store_ref.shape[0]
    heads = segments
    share = v_ref.shape[1] // q_ref.shape[1]

    barrier = pltpu.get_barrier_semaphore()

    def greet_row(step, carry):
        other = lax.rem(col + step, columns)
        pl.semaphore_signal(barrier, inc=1, device_id=(seg, other), device_id_type=MESH)
        return carry

    def greet_line(step, carry):
        other = lax.rem(seg + step, segments)
        pl.semaphore_signal(barrier, inc=1, device_id=(other, col), device_id_type=MESH)
        return carry

    lax.fori_loop(1, columns, greet_row, 0)
    lax.fori_loop(1, segments, greet_line, 0)
    pl.semaphore_wait(barrier, columns + segments - 2)

    def propose(i, carry):
        other = lax.rem(col + i, columns)
        wanted = row_ref[other]
        block = jnp.zeros((dim, dim), jnp.float32)
        for r in range(cached):
            match = jnp.where(wanted == col * cached + r, 1.0, 0.0)
            block = block + store_ref[r, 0].astype(jnp.float32) * match
        offer[other] = block.astype(jnp.bfloat16)

        @pl.when(i == 0)
        def _():
            pltpu.make_async_copy(offer.at[col], taken.at[col], taken_recv).start()

        @pl.when(i > 0)
        def _():
            pltpu.make_async_remote_copy(
                src_ref=offer.at[other],
                dst_ref=taken.at[col],
                send_sem=offer_send,
                recv_sem=taken_recv,
                device_id=(seg, other),
                device_id_type=MESH,
            ).start()

        return carry

    lax.fori_loop(0, columns, propose, 0)

    line = lax.broadcasted_iota(jnp.int32, (tok, tok), 0)
    lane = lax.broadcasted_iota(jnp.int32, (tok, tok), 1)
    place = lax.broadcasted_iota(jnp.int32, (tok, 1), 0)
    valid = jnp.where(place + seg * tok < len_ref[0], 1.0, 0.0)
    strength_ref[...] = beta_ref[...].astype(jnp.float32) * valid
    logs = (decay_ref[...].astype(jnp.float32) * valid).astype(jnp.bfloat16)
    lower = jnp.where(line >= lane, 1.0, 0.0).astype(jnp.bfloat16)
    upper = jnp.where(line <= lane, 1.0, 0.0).astype(jnp.bfloat16)
    total_ref[...] = jnp.dot(lower, logs, preferred_element_type=jnp.float32)
    across_ref[...] = lax.dot_general(
        logs, upper, (((0,), (0,)), ((), ())), preferred_element_type=jnp.float32
    )
    identity = jnp.where(line == lane, 1.0, 0.0)
    which = lax.broadcasted_iota(jnp.int32, (tok, heads), 1)

    def column_of(ref, j):
        return jnp.sum(jnp.where(which == j, ref[...], 0.0), axis=1, keepdims=True)

    def local_work(i, carry):
        spot = pl.ds(pl.multiple_of(i * dim, dim), dim)
        keys = unit_rows(k_ref[:, spot].astype(jnp.float32), 1.0)
        queries = unit_rows(q_ref[:, spot].astype(jnp.float32), dim ** (-0.5))
        keys_across = keys.T
        grams = paired_dot(
            left_pair(jnp.concatenate([keys, queries], axis=0)), right_pair(keys_across)
        )
        for a in range(share):
            j = i * share + a
            strength = column_of(strength_ref, j)
            total = column_of(total_ref, j)
            across = across_ref[pl.ds(j, 1), :]
            last = across[:, tok - 1 :]
            values = v_ref[:, pl.ds(pl.multiple_of(j * dim, dim), dim)].astype(jnp.float32)
            spread = total - across
            upto = jnp.where(line >= lane, jnp.exp(jnp.where(line >= lane, spread, 0.0)), 0.0)
            coupling = jnp.where(line > lane, strength * upto * grams[:tok], 0.0)
            inverse = identity - jnp.where((line == lane + 1) & (line % 2 == 1), coupling, 0.0)
            size = 2
            while size < tok:
                corner = (
                    (line // (2 * size) == lane // (2 * size))
                    & ((line // size) % 2 == 1)
                    & ((lane // size) % 2 == 0)
                )
                inner = paired_dot(
                    left_pair(jnp.where(corner, coupling, 0.0)), right_pair(inverse)
                )
                inverse = inverse - paired_dot(left_pair(inverse), right_pair(inner))
                size *= 2
            growth = jnp.exp(total)
            solver = left_pair(inverse)
            pseudo = right_pair(paired_dot(solver, right_pair(strength * values)))
            weights = right_pair(paired_dot(solver, right_pair((strength * growth) * keys)))
            tail = keys_across * jnp.exp(last - across)
            scores = upto * grams[tok:]
            left = left_pair(jnp.concatenate([tail, scores], axis=0))
            minus = paired_dot(left, weights)
            step_add[j] = paired_dot(left, pseudo)
            step_left[j] = left_pair(
                jnp.concatenate([jnp.exp(last) * identity, growth * queries], axis=0) - minus
            )
        return carry

    def hand_on(j, carry):
        return pltpu.make_async_remote_copy(
            src_ref=passed.at[j],
            dst_ref=held.at[j],
            send_sem=passed_send.at[j],
            recv_sem=held_recv.at[j],
            device_id=(seg + 1, col),
            device_id_type=MESH,
        )

    def origin_copy():
        return pltpu.make_async_remote_copy(
            src_ref=origin,
            dst_ref=held.at[seg],
            send_sem=origin_send,
            recv_sem=held_recv.at[seg],
            device_id=(0, col),
            device_id_type=MESH,
        )

    def end_copy(j):
        return pltpu.make_async_remote_copy(
            src_ref=ends.at[j],
            dst_ref=final_ref,
            send_sem=ends_send.at[j],
            recv_sem=final_recv,
            device_id=(j, col),
            device_id_type=MESH,
        )

    def give_origin():
        pltpu.make_async_copy(taken, taken, taken_recv).wait()

        def add_up(i, block):
            return block + taken[i].astype(jnp.float32)

        origin[...] = lax.fori_loop(0, columns, add_up, jnp.zeros((dim, dim), jnp.float32))

        @pl.when(seg == 0)
        def _():
            pltpu.make_async_copy(origin, held.at[0], held_recv.at[0]).start()

        @pl.when(seg > 0)
        def _():
            origin_copy().start()

    def local_step(i, carry):
        local_work(i, carry)

        @pl.when(i == heads // share // 2)
        def _():
            give_origin()

        return carry

    lax.fori_loop(0, heads // share, local_step, 0)

    def chain(j, carry):
        pltpu.make_async_copy(held.at[j], held.at[j], held_recv.at[j]).wait()
        state = right_pair(held[j])
        passed[j] = paired_dot(step_left[j, :dim], state) + step_add[j, :dim]

        @pl.when(seg < segments - 1)
        def _():
            hand_on(j, 0).start()

        @pl.when(seg == segments - 1)
        def _():
            ends[j] = passed[j].astype(jnp.bfloat16)

            @pl.when(j < segments - 1)
            def _():
                end_copy(j).start()

            @pl.when(j == segments - 1)
            def _():
                pltpu.make_async_copy(ends.at[j], final_ref, final_recv).start()

        raw = (paired_dot(step_left[j, dim:], state) + step_add[j, dim:]) * valid
        squares = jnp.sum(raw * raw, axis=-1, keepdims=True) * (1.0 / dim)
        normed = raw * lax.rsqrt(squares + 1e-06) * gain_ref[...]
        mixed_ref[:, pl.ds(pl.multiple_of(j * dim, dim), dim)] = normed.astype(jnp.bfloat16)
        tall[pl.ds(j, tok, stride=heads), :] = normed
        return carry

    lax.fori_loop(0, heads, chain, 0)
    rows_ref[...] = tall[...].astype(jnp.bfloat16).reshape(tok, heads, dim)
    pltpu.make_async_copy(final_ref, final_ref, final_recv).wait()

    sent = offer.at[pl.ds(0, columns - 1)]
    pltpu.make_async_copy(sent, sent, offer_send).wait()

    @pl.when(seg > 0)
    def _():
        origin_copy().wait_send()

    def drain(j, carry):
        @pl.when(seg < segments - 1)
        def _():
            hand_on(j, 0).wait_send()

        @pl.when((seg == segments - 1) & (j < segments - 1))
        def _():
            end_copy(j).wait_send()

        return carry

    lax.fori_loop(0, heads, drain, 0)


def delta(suffix_len, cache_row, q, k, v, beta, decay, gain, store):
    segments = lax.axis_size("segment")
    columns = lax.axis_size("expert")
    tok, width = v.shape
    dim = store.shape[-1]
    heads = segments
    bf, f32 = jnp.bfloat16, jnp.float32
    dma = pltpu.SemaphoreType.DMA
    whole = pl.BlockSpec(memory_space=pltpu.VMEM)
    scalars = pl.BlockSpec(memory_space=pltpu.SMEM)
    return pl.pallas_call(
        delta_kernel,
        out_shape=(
            jax.ShapeDtypeStruct((tok, width), bf),
            jax.ShapeDtypeStruct((tok, heads, dim), bf),
            jax.ShapeDtypeStruct((dim, dim), bf),
        ),
        in_specs=[scalars, scalars] + [whole] * 7,
        out_specs=(whole, whole, whole),
        scratch_shapes=[
            pltpu.VMEM((columns, dim, dim), bf),
            pltpu.VMEM((columns, dim, dim), bf),
            pltpu.VMEM((dim, dim), f32),
            pltpu.VMEM((heads, dim, dim), f32),
            pltpu.VMEM((heads, dim, dim), f32),
            pltpu.VMEM((heads, 2 * dim, 2 * dim), bf),
            pltpu.VMEM((heads, 2 * dim, dim), f32),
            pltpu.VMEM((heads, dim, dim), bf),
            pltpu.VMEM((tok * heads, dim), f32),
            pltpu.VMEM((tok, heads), f32),
            pltpu.VMEM((tok, heads), f32),
            pltpu.VMEM((heads, tok), f32),
            dma,
            dma,
            dma,
            dma((heads,)),
            dma((heads,)),
            dma((heads,)),
            dma,
        ],
        compiler_params=pltpu.CompilerParams(
            collective_id=2, has_side_effects=True, vmem_limit_bytes=40 * 1024 * 1024
        ),
    )(suffix_len, cache_row, q, k, v, beta, decay, gain, store)


def moe_kernel(
    idx_ref,
    rows_ref,
    base_ref,
    mix_ref,
    gate_ref,
    up_ref,
    down_ref,
    out_ref,
    climb,
    sink,
    pick,
    stage,
    arrive,
    back,
    flat,
    sum_up,
    sum_down,
    got_up,
    got_down,
    tall,
    wide,
    climb_send,
    climb_recv,
    sink_send,
    sink_recv,
    stage_send,
    arrive_recv,
    back_send,
    back_recv,
    up_send,
    up_recv,
    down_send,
    down_recv,
):
    segments = lax.axis_size("segment")
    columns = lax.axis_size("expert")
    pairs = segments // 2
    tok = rows_ref.shape[0]
    heads = rows_ref.shape[1]
    lane = rows_ref.shape[2]
    half = tok // 2
    seg = lax.axis_index("segment")
    col = lax.axis_index("expert")
    above = lax.rem(seg + 1, segments)
    below = lax.rem(seg + segments - 1, segments)

    barrier = pltpu.get_barrier_semaphore()

    def greet(step, carry):
        other = lax.rem(col + step, columns)
        pl.semaphore_signal(barrier, inc=1, device_id=(seg, other), device_id_type=MESH)
        return carry

    lax.fori_loop(1, columns, greet, 0)
    pl.semaphore_signal(barrier, inc=1, device_id=(above, col), device_id_type=MESH)
    pl.semaphore_signal(barrier, inc=1, device_id=(below, col), device_id_type=MESH)
    pl.semaphore_wait(barrier, columns + 1)

    def part(ref, h):
        return ref.at[pl.ds(h * half, half)]

    def climb_copy(source, slot, h):
        return pltpu.make_async_remote_copy(
            src_ref=part(source, h),
            dst_ref=part(climb.at[slot], h),
            send_sem=climb_send.at[slot, h],
            recv_sem=climb_recv.at[slot, h],
            device_id=(above, col),
            device_id_type=MESH,
        )

    def sink_copy(source, slot, h):
        return pltpu.make_async_remote_copy(
            src_ref=part(source, h),
            dst_ref=part(sink.at[slot], h),
            send_sem=sink_send.at[slot, h],
            recv_sem=sink_recv.at[slot, h],
            device_id=(below, col),
            device_id_type=MESH,
        )

    for h in range(2):
        climb_copy(rows_ref, 0, h).start()
        sink_copy(rows_ref, 1, h).start()
    sink[0] = rows_ref[...]

    def rows_to_wide(rows):
        tall[...] = rows.reshape(tok * heads, lane).astype(jnp.float32)
        for j in range(heads):
            wide[:, j * lane : (j + 1) * lane] = tall[pl.ds(j, tok, stride=heads), :].astype(
                jnp.bfloat16
            )

    def send_out(source, target, send_sem, recv_sem, p, i):
        other = lax.rem(col + i, columns)

        @pl.when(i == 0)
        def _():
            pltpu.make_async_copy(source.at[p, col], target.at[p, col], recv_sem.at[p]).start()

        @pl.when(i > 0)
        def _():
            pltpu.make_async_remote_copy(
                src_ref=source.at[p, other],
                dst_ref=target.at[p, col],
                send_sem=send_sem.at[p],
                recv_sem=recv_sem.at[p],
                device_id=(seg, other),
                device_id_type=MESH,
            ).start()

    def wait_all(target, sem, p):
        pltpu.make_async_copy(target.at[p], target.at[p], sem.at[p]).wait()

    def wait_sent(source, sem, p):
        piece = source.at[p, pl.ds(0, columns - 1)]
        pltpu.make_async_copy(piece, piece, sem.at[p]).wait()

    def dispatch(p):
        pick[0] = sink[p]
        pick[1] = climb[p]

        def one(i, carry):
            other = lax.rem(col + i, columns)
            for r in range(4):
                stage[p, other, r] = pick[r // 2, idx_ref[p, other, r]]
            send_out(stage, arrive, stage_send, arrive_recv, p, i)
            return carry

        lax.fori_loop(0, columns, one, 0)

    def experts(p):
        wait_all(arrive, arrive_recv, p)
        wait_sent(stage, stage_send, p)
        rows_to_wide(arrive[p].reshape(tok, heads, lane))
        gate_part = jnp.dot(wide[...], gate_ref[...], preferred_element_type=jnp.float32)
        up_part = jnp.dot(wide[...], up_ref[...], preferred_element_type=jnp.float32)
        hidden = (gate_part * jax.nn.sigmoid(gate_part) * up_part).astype(jnp.bfloat16)
        for j in range(heads):
            tall[pl.ds(j, tok, stride=heads), :] = jnp.dot(
                hidden,
                down_ref[:, j * lane : (j + 1) * lane],
                preferred_element_type=jnp.float32,
            )
        stage[p] = tall[...].astype(jnp.bfloat16).reshape(columns, 4, heads, lane)

        def one(i, carry):
            send_out(stage, back, back_send, back_recv, p, i)
            return carry

        lax.fori_loop(0, columns, one, 0)

    def land(p):
        wait_all(back, back_recv, p)
        rows_to_wide(back[p].reshape(tok, heads, lane))
        flat[p] = wide[...]

    def gather_step(p, carry):
        for h in range(2):
            climb_copy(rows_ref, p, h).wait_recv()

            @pl.when(p < pairs - 1)
            def _():
                climb_copy(climb.at[p], p + 1, h).start()

            @pl.when(p >= 1)
            def _():
                sink_copy(rows_ref, p, h).wait_recv()

                @pl.when(p < pairs - 1)
                def _():
                    sink_copy(sink.at[p], p + 1, h).start()

        dispatch(p)

        @pl.when(p >= 1)
        def _():
            experts(p - 1)

        @pl.when(p >= 2)
        def _():
            land(p - 2)

        return carry

    lax.fori_loop(0, pairs, gather_step, 0)
    experts(pairs - 1)
    land(pairs - 2)
    land(pairs - 1)

    def term(p, source, h):
        weights = mix_ref[p, source, pl.ds(h * half, half), :]
        rows = flat[p]
        slots = rows.shape[0]
        return jnp.dot(
            weights[:, :slots], rows, preferred_element_type=jnp.float32
        ) + jnp.dot(weights[:, slots:], rows, preferred_element_type=jnp.float32)

    def up_copy(i, h):
        return pltpu.make_async_remote_copy(
            src_ref=part(sum_up.at[i], h),
            dst_ref=part(got_up.at[i], h),
            send_sem=up_send.at[i, h],
            recv_sem=up_recv.at[i, h],
            device_id=(above, col),
            device_id_type=MESH,
        )

    def down_copy(i, h):
        return pltpu.make_async_remote_copy(
            src_ref=part(sum_down.at[i], h),
            dst_ref=part(got_down.at[i], h),
            send_sem=down_send.at[i, h],
            recv_sem=down_recv.at[i, h],
            device_id=(below, col),
            device_id_type=MESH,
        )

    for h in range(2):
        spot = pl.ds(h * half, half)
        sum_up[0, spot] = term(pairs - 1, 1, h).astype(jnp.bfloat16)
        up_copy(0, h).start()
        sum_down[0, spot] = term(pairs - 2, 1, h).astype(jnp.bfloat16)
        down_copy(0, h).start()

    def reduce_step(i, carry):
        for h in range(2):
            spot = pl.ds(h * half, half)
            mine = term(pairs - i, 0, h)
            up_copy(i - 1, h).wait_recv()
            sum_up[i, spot] = (mine + got_up[i - 1, spot].astype(jnp.float32)).astype(jnp.bfloat16)
            up_copy(i, h).start()

            @pl.when(i < pairs - 1)
            def _():
                mine = term(pairs - 2 - i, 1, h)
                down_copy(i - 1, h).wait_recv()
                sum_down[i, spot] = (mine + got_down[i - 1, spot].astype(jnp.float32)).astype(
                    jnp.bfloat16
                )
                down_copy(i, h).start()

        return carry

    lax.fori_loop(1, pairs, reduce_step, 0)
    for h in range(2):
        spot = pl.ds(h * half, half)
        total = base_ref[spot, :].astype(jnp.float32) + term(0, 0, h)
        down_copy(pairs - 2, h).wait_recv()
        total = total + got_down[pairs - 2, spot].astype(jnp.float32)
        up_copy(pairs - 1, h).wait_recv()
        total = total + got_up[pairs - 1, spot].astype(jnp.float32)
        out_ref[spot, :] = total.astype(jnp.bfloat16)

    def drain(p, carry):
        wait_sent(stage, back_send, p)
        for h in range(2):
            climb_copy(rows_ref, p, h).wait_send()
            up_copy(p, h).wait_send()

            @pl.when(p >= 1)
            def _():
                sink_copy(rows_ref, p, h).wait_send()
                down_copy(p - 1, h).wait_send()

        return carry

    lax.fori_loop(0, pairs, drain, 0)


def moe(idx, rows, base, mix, w_gate, w_up, w_down):
    segments = lax.axis_size("segment")
    columns = lax.axis_size("expert")
    pairs = segments // 2
    tok, heads, lane = rows.shape
    width = base.shape[1]
    slots = columns * 4
    bf = jnp.bfloat16
    dma = pltpu.SemaphoreType.DMA
    whole = pl.BlockSpec(memory_space=pltpu.VMEM)
    return pl.pallas_call(
        moe_kernel,
        out_shape=jax.ShapeDtypeStruct((tok, width), bf),
        in_specs=[pl.BlockSpec(memory_space=pltpu.SMEM)] + [whole] * 6,
        out_specs=whole,
        scratch_shapes=[
            pltpu.VMEM((pairs, tok, heads, lane), bf),
            pltpu.VMEM((pairs, tok, heads, lane), bf),
            pltpu.VMEM((2, tok, heads, lane), bf),
            pltpu.VMEM((pairs, columns, 4, heads, lane), bf),
            pltpu.VMEM((pairs, columns, 4, heads, lane), bf),
            pltpu.VMEM((pairs, columns, 4, heads, lane), bf),
            pltpu.VMEM((pairs, slots, width), bf),
            pltpu.VMEM((pairs, tok, width), bf),
            pltpu.VMEM((pairs - 1, tok, width), bf),
            pltpu.VMEM((pairs, tok, width), bf),
            pltpu.VMEM((pairs - 1, tok, width), bf),
            pltpu.VMEM((tok * heads, lane), jnp.float32),
            pltpu.VMEM((tok, width), bf),
            dma((pairs, 2)),
            dma((pairs, 2)),
            dma((pairs, 2)),
            dma((pairs, 2)),
            dma((pairs,)),
            dma((pairs,)),
            dma((pairs,)),
            dma((pairs,)),
            dma((pairs, 2)),
            dma((pairs, 2)),
            dma((pairs - 1, 2)),
            dma((pairs - 1, 2)),
        ],
        compiler_params=pltpu.CompilerParams(
            collective_id=1, has_side_effects=True, vmem_limit_bytes=60 * 1024 * 1024
        ),
    )(idx, rows, base, mix, w_gate, w_up, w_down)


def route_tables(expert_ids, route_weight):
    segments = lax.axis_size("segment")
    columns = lax.axis_size("expert")
    seg = lax.axis_index("segment")
    pairs = segments // 2
    tok, top = expert_ids.shape
    routes = jnp.concatenate([expert_ids.T.astype(jnp.float32), route_weight.T], axis=0)
    routes = lax.all_gather(routes, "segment", axis=0, tiled=False)
    step = jnp.arange(pairs, dtype=jnp.int32)
    place = jnp.stack([seg + step, seg + segments - 1 - step], axis=1) % segments
    routes = routes[place]
    here = (seg * columns + jnp.arange(columns, dtype=jnp.int32)).astype(jnp.float32)
    same = routes[:, :, None, :top, :] == here[None, None, :, None, None]
    weight = jnp.sum(jnp.where(same, routes[:, :, None, top:, :], 0.0), axis=3)
    named = jnp.any(same, axis=3)
    token = jnp.arange(tok, dtype=jnp.int32)
    first = jnp.min(jnp.where(named, token, tok), axis=-1)
    last = jnp.max(jnp.where(named, token, -1), axis=-1)
    index = jnp.stack([first % tok, jnp.maximum(last, 0)], axis=-1)
    index = index.transpose(0, 2, 1, 3).reshape(pairs, columns, 4)
    at_first = jnp.where(token == first[..., None], weight, 0.0)
    at_last = jnp.where((token == last[..., None]) & (last != first)[..., None], weight, 0.0)
    both = jnp.stack([at_first, at_last], axis=3)
    none = jnp.zeros_like(both[:, 0])
    mix = jnp.stack(
        [
            jnp.concatenate([both[:, 0], none], axis=2),
            jnp.concatenate([none, both[:, 1]], axis=2),
        ],
        axis=1,
    )
    mix = mix.reshape(pairs, 2, columns * 4, tok).transpose(0, 1, 3, 2)
    high = lax.reduce_precision(mix, 8, 7)
    low = lax.reduce_precision(mix - high, 8, 7)
    mix = jnp.concatenate([high, low], axis=-1).astype(jnp.bfloat16)
    return index, mix


def shards(
    q_heads,
    k_heads,
    values,
    beta,
    decay,
    head_gain,
    suffix_len,
    store_states,
    cache_row,
    write_slot,
    expert_ids,
    route_weight,
    w_gate,
    w_up,
    w_down,
):
    mixed, rows, final = delta(
        suffix_len,
        cache_row,
        q_heads[0],
        k_heads[0],
        values[0],
        beta[0],
        decay[0],
        head_gain.reshape(1, -1),
        store_states,
    )
    index, mix = route_tables(expert_ids[0], route_weight[0])
    store_out = lax.dynamic_update_index_in_dim(store_states, final[None], write_slot[0], 0)
    out = moe(index, rows, mixed, mix, w_gate[0], w_up[0], w_down[0])
    return (out[None], store_out)


def solution(mesh):
    return jax.shard_map(
        shards,
        mesh=mesh,
        in_specs=(
            P("expert", "segment", None),
            P("expert", "segment", None),
            P("expert", "segment", None),
            P("expert", "segment", None),
            P("expert", "segment", None),
            P(),
            P("expert"),
            P("expert", "segment", None, None),
            P(),
            P("expert"),
            P("expert", "segment", None),
            P("expert", "segment", None),
            P(("segment", "expert"), None, None),
            P(("segment", "expert"), None, None),
            P(("segment", "expert"), None, None),
        ),
        out_specs=(P("expert", "segment", None), P("expert", "segment", None, None)),
        check_vma=False,
    )
```

```python
import jax
import jax.numpy as jnp
from jax import lax
from jax.experimental import pallas as pl
from jax.experimental.pallas import tpu as pltpu
from jax.sharding import PartitionSpec as P

MESH = pl.DeviceIdType.MESH


GROUP = 4


def halves(block):
    high = block.astype(jnp.bfloat16)
    low = (block - high.astype(jnp.float32)).astype(jnp.bfloat16)
    return high, low


def left_pair(block):
    high, low = halves(block)
    return jnp.concatenate([high, low], axis=1)


def right_pair(block):
    high, low = halves(block)
    row = jnp.concatenate([high, low], axis=1)
    return jnp.concatenate([row, row], axis=0)


def paired_dot(left, right):
    both = jnp.dot(left, right, preferred_element_type=jnp.float32)
    width = both.shape[1] // 2
    return both[:, :width] + both[:, width:]


def unit_rows(block, factor):
    squares = jnp.sum(block * block, axis=-1, keepdims=True)
    return block * (lax.rsqrt(squares + 1e-06) * factor)


def mixer_kernel(
    len_ref,
    row_ref,
    slot_ref,
    beta_ref,
    decay_ref,
    gain_ref,
    ids_ref,
    weight_ref,
    store_in,
    k_in,
    q_in,
    v_in,
    gate_in,
    up_in,
    down_in,
    out_ref,
    store_out_ref,
    store_ref,
    k_ref,
    q_ref,
    v_ref,
    gate_ref,
    up_ref,
    down_ref,
    routes_ref,
    routes_all,
    index_ref,
    idx_ref,
    mix_ref,
    spread_ref,
    mixed_ref,
    rows_ref,
    final_ref,
    offer,
    taken,
    origin,
    held,
    passed,
    step_left,
    step_add,
    strength_ref,
    total_ref,
    across_ref,
    climb,
    sink,
    distant,
    pick,
    stage,
    arrive,
    back,
    flat,
    sum_up,
    sum_down,
    got_up,
    got_down,
    tall,
    wide,
    load_sem,
    routes_send,
    routes_recv,
    index_sem,
    offer_send,
    taken_recv,
    origin_send,
    held_recv,
    passed_send,
    ends_send,
    final_recv,
    distant_send,
    distant_recv,
    climb_send,
    climb_recv,
    sink_send,
    sink_recv,
    stage_send,
    arrive_recv,
    back_send,
    back_recv,
    up_send,
    up_recv,
    down_send,
    down_recv,
):
    segments = lax.axis_size("segment")
    columns = lax.axis_size("expert")
    seg = lax.axis_index("segment")
    col = lax.axis_index("expert")
    pairs = segments // 2
    tok = q_ref.shape[0]
    half = tok // 2
    dim = store_ref.shape[-1]
    cached = store_ref.shape[0]
    heads = segments
    share = v_ref.shape[1] // q_ref.shape[1]
    top = ids_ref.shape[0]
    above = lax.rem(seg + 1, segments)
    below = lax.rem(seg + segments - 1, segments)

    def load(source, target, k):
        return pltpu.make_async_copy(source, target, load_sem.at[k])

    for k, (source, target) in enumerate(
        (
            (store_in, store_ref),
            (k_in, k_ref),
            (q_in, q_ref),
            (v_in, v_ref),
            (gate_in, gate_ref),
            (up_in, up_ref),
            (down_in, down_ref),
        )
    ):
        load(source, target, k).start()
    routes_ref[:top] = ids_ref[...].astype(jnp.float32)
    routes_ref[top:] = weight_ref[...]

    barrier = pltpu.get_barrier_semaphore()

    def greet_row(step, carry):
        other = lax.rem(col + step, columns)
        pl.semaphore_signal(barrier, inc=1, device_id=(seg, other), device_id_type=MESH)
        return carry

    def greet_line(step, carry):
        other = lax.rem(seg + step, segments)
        pl.semaphore_signal(barrier, inc=1, device_id=(other, col), device_id_type=MESH)
        return carry

    lax.fori_loop(1, columns, greet_row, 0)
    lax.fori_loop(1, segments, greet_line, 0)
    pl.semaphore_wait(barrier, columns + segments - 2)

    far = segments // 2
    pltpu.make_async_copy(routes_ref, routes_all.at[0], routes_recv).start()

    def routes_copy(step, slot):
        return pltpu.make_async_remote_copy(
            src_ref=routes_ref,
            dst_ref=routes_all.at[slot],
            send_sem=routes_send.at[slot],
            recv_sem=routes_recv,
            device_id=(lax.rem(seg + step, segments), col),
            device_id_type=MESH,
        )

    def routes_out(k, carry):
        routes_copy(k, 2 * k - 1).start()
        routes_copy(segments - k, 2 * k).start()
        return carry

    lax.fori_loop(1, far, routes_out, 0)
    routes_copy(far, segments - 1).start()

    load(store_in, store_ref, 0).wait()

    def propose(i, carry):
        other = lax.rem(col + i, columns)
        wanted = row_ref[other]
        block = jnp.zeros((dim, dim), jnp.float32)
        for r in range(cached):
            match = jnp.where(wanted == col * cached + r, 1.0, 0.0)
            block = block + store_ref[r, 0].astype(jnp.float32) * match
        offer[other] = block.astype(jnp.bfloat16)

        @pl.when(i == 0)
        def _():
            pltpu.make_async_copy(offer.at[col], taken.at[col], taken_recv).start()

        @pl.when(i > 0)
        def _():
            pltpu.make_async_remote_copy(
                src_ref=offer.at[other],
                dst_ref=taken.at[col],
                send_sem=offer_send,
                recv_sem=taken_recv,
                device_id=(seg, other),
                device_id_type=MESH,
            ).start()

        return carry

    lax.fori_loop(0, columns, propose, 0)

    line = lax.broadcasted_iota(jnp.int32, (tok, tok), 0)
    lane = lax.broadcasted_iota(jnp.int32, (tok, tok), 1)
    place = lax.broadcasted_iota(jnp.int32, (tok, 1), 0)
    valid = jnp.where(place + seg * tok < len_ref[0], 1.0, 0.0)
    along = lax.broadcasted_iota(jnp.int32, (1, tok), 1)
    valid_along = jnp.where(along + seg * tok < len_ref[0], 1.0, 0.0)
    logs = (decay_ref[...].astype(jnp.float32) * valid_along).astype(jnp.bfloat16)
    writes = (beta_ref[...].astype(jnp.float32) * valid_along).astype(jnp.bfloat16)
    lower = jnp.where(line >= lane, 1.0, 0.0).astype(jnp.bfloat16)
    upper = jnp.where(line <= lane, 1.0, 0.0).astype(jnp.bfloat16)
    diagonal = jnp.where(line == lane, 1.0, 0.0).astype(jnp.bfloat16)
    turned = (((1,), (1,)), ((), ()))
    across_ref[...] = jnp.dot(logs, upper, preferred_element_type=jnp.float32)
    total_ref[...] = lax.dot_general(lower, logs, turned, preferred_element_type=jnp.float32)
    strength_ref[...] = lax.dot_general(
        diagonal, writes, turned, preferred_element_type=jnp.float32
    )
    for k, (source, target) in enumerate(((k_in, k_ref), (q_in, q_ref), (v_in, v_ref))):
        load(source, target, k + 1).wait()
    identity = jnp.where(line == lane, 1.0, 0.0)
    which = lax.broadcasted_iota(jnp.int32, (tok, heads), 1)

    def column_of(ref, j):
        return jnp.sum(jnp.where(which == j, ref[...], 0.0), axis=1, keepdims=True)

    def local_work(i, carry):
        grams, across_keys, unit_keys, unit_queries = [], [], [], []
        for g in range(GROUP):
            spot = pl.ds(pl.multiple_of((i * GROUP + g) * dim, dim), dim)
            keys = unit_rows(k_ref[:, spot].astype(jnp.float32), 1.0)
            queries = unit_rows(q_ref[:, spot].astype(jnp.float32), dim ** (-0.5))
            unit_keys.append(keys)
            unit_queries.append(queries)
            across_keys.append(keys.T)
        for g in range(GROUP):
            grams.append(
                paired_dot(
                    left_pair(jnp.concatenate([unit_keys[g], unit_queries[g]], axis=0)),
                    right_pair(across_keys[g]),
                )
            )
        count = GROUP * share
        number = [i * count + a for a in range(count)]
        strength = [column_of(strength_ref, j) for j in number]
        total = [column_of(total_ref, j) for j in number]
        across = [across_ref[pl.ds(j, 1), :] for j in number]
        upto = [
            jnp.where(line >= lane, jnp.exp(jnp.where(line >= lane, total[a] - across[a], 0.0)), 0.0)
            for a in range(count)
        ]
        coupling = [
            jnp.where(line > lane, strength[a] * upto[a] * grams[a // share][:tok], 0.0)
            for a in range(count)
        ]
        inverse = [
            identity - jnp.where((line == lane + 1) & (line % 2 == 1), coupling[a], 0.0)
            for a in range(count)
        ]
        size = 2
        while size < tok:
            corner = (
                (line // (2 * size) == lane // (2 * size))
                & ((line // size) % 2 == 1)
                & ((lane // size) % 2 == 0)
            )
            inner = [
                paired_dot(
                    left_pair(jnp.where(corner, coupling[a], 0.0)), right_pair(inverse[a])
                )
                for a in range(count)
            ]
            inverse = [
                inverse[a] - paired_dot(left_pair(inverse[a]), right_pair(inner[a]))
                for a in range(count)
            ]
            size *= 2
        growth = [jnp.exp(total[a]) for a in range(count)]
        solver = [left_pair(inverse[a]) for a in range(count)]
        pseudo = []
        for a in range(count):
            spot = pl.ds(pl.multiple_of(number[a] * dim, dim), dim)
            values = v_ref[:, spot].astype(jnp.float32)
            pseudo.append(right_pair(paired_dot(solver[a], right_pair(strength[a] * values))))
        weights = [
            right_pair(
                paired_dot(solver[a], right_pair((strength[a] * growth[a]) * unit_keys[a // share]))
            )
            for a in range(count)
        ]
        for a in range(count):
            last = across[a][:, tok - 1 :]
            tail = across_keys[a // share] * jnp.exp(last - across[a])
            scores = upto[a] * grams[a // share][tok:]
            left = left_pair(jnp.concatenate([tail, scores], axis=0))
            minus = paired_dot(left, weights[a])
            step_add[number[a]] = paired_dot(left, pseudo[a])
            step_left[number[a]] = left_pair(
                jnp.concatenate(
                    [jnp.exp(last) * identity, growth[a] * unit_queries[a // share]], axis=0
                )
                - minus
            )
        return carry

    def hand_on(j, carry):
        return pltpu.make_async_remote_copy(
            src_ref=passed.at[j],
            dst_ref=held.at[j],
            send_sem=passed_send.at[j],
            recv_sem=held_recv.at[j],
            device_id=(seg + 1, col),
            device_id_type=MESH,
        )

    def origin_copy():
        return pltpu.make_async_remote_copy(
            src_ref=origin,
            dst_ref=held.at[seg],
            send_sem=origin_send,
            recv_sem=held_recv.at[seg],
            device_id=(0, col),
            device_id_type=MESH,
        )

    def end_copy(j):
        return pltpu.make_async_remote_copy(
            src_ref=passed.at[j],
            dst_ref=final_ref,
            send_sem=ends_send.at[j],
            recv_sem=final_recv,
            device_id=(j, col),
            device_id_type=MESH,
        )

    def give_origin():
        pltpu.make_async_copy(taken, taken, taken_recv).wait()

        def add_up(i, block):
            return block + taken[i].astype(jnp.float32)

        block = lax.fori_loop(0, columns, add_up, jnp.zeros((dim, dim), jnp.float32))
        origin[:, :dim] = block.astype(jnp.bfloat16)
        origin[:, dim:] = jnp.zeros((dim, dim), jnp.bfloat16)

        @pl.when(seg == 0)
        def _():
            pltpu.make_async_copy(origin, held.at[0], held_recv.at[0]).start()

        @pl.when(seg > 0)
        def _():
            origin_copy().start()

    def local_step(i, carry):
        local_work(i, carry)

        @pl.when(i == heads // share // GROUP // 2)
        def _():
            give_origin()

        return carry

    lax.fori_loop(0, heads // share // GROUP, local_step, 0)

    names = lax.broadcasted_iota(jnp.int32, (columns, 1), 0) + seg * columns
    token = lax.broadcasted_iota(jnp.int32, (columns, tok), 1)

    def locate(slot):
        routes = routes_all[slot]
        top = routes.shape[0] // 2
        weight = jnp.zeros((columns, tok), jnp.float32)
        first = jnp.full((columns, tok), tok, jnp.int32)
        last = jnp.full((columns, tok), -1, jnp.int32)
        for k in range(top):
            same = routes[k : k + 1, :].astype(jnp.int32) == names
            weight = weight + jnp.where(same, routes[top + k : top + k + 1, :], 0.0)
            first = jnp.where(same, token, first)
            last = jnp.where(same, token, last)
        first = jnp.min(first, axis=1, keepdims=True)
        last = jnp.max(last, axis=1, keepdims=True)
        index_ref[slot] = jnp.where(token == 0, jnp.where(first < tok, first, 0), jnp.maximum(last, 0))
        pltpu.make_async_copy(index_ref.at[slot], idx_ref.at[slot], index_sem).start()
        at_first = jnp.where(token == first, weight, 0.0)
        at_last = jnp.where((token == last) & (last != first), weight, 0.0)
        return at_first, at_last

    def tabulate(slot, p, source, width):
        at_first, at_last = locate(slot)
        spread_ref[...] = jnp.zeros_like(spread_ref)
        spread_ref[pl.ds(2 * source, columns, stride=width), :] = at_first
        spread_ref[pl.ds(2 * source + 1, columns, stride=width), :] = at_last
        mix_ref[p, source] = left_pair(spread_ref[...].T)

    def chain(j, carry):
        pltpu.make_async_copy(held.at[j], held.at[j], held_recv.at[j]).wait()
        state = jnp.concatenate([held[j], held[j]], axis=0)
        passed[j] = left_pair(paired_dot(step_left[j, :dim], state) + step_add[j, :dim])

        @pl.when(seg < segments - 1)
        def _():
            hand_on(j, 0).start()

        @pl.when((seg == segments - 1) & (j < segments - 1))
        def _():
            end_copy(j).start()

        @pl.when((seg == segments - 1) & (j == segments - 1))
        def _():
            pltpu.make_async_copy(passed.at[j], final_ref, final_recv).start()

        raw = (paired_dot(step_left[j, dim:], state) + step_add[j, dim:]) * valid
        squares = jnp.sum(raw * raw, axis=-1, keepdims=True) * (1.0 / dim)
        normed = raw * lax.rsqrt(squares + 1e-06) * gain_ref[...]
        mixed_ref[:, pl.ds(pl.multiple_of(j * dim, dim), dim)] = normed.astype(jnp.bfloat16)
        tall[pl.ds(j, tok, stride=heads), :] = normed

        @pl.when(j == 0)
        def _():
            pltpu.make_async_copy(routes_all, routes_all, routes_recv).wait()
            tabulate(0, 0, 0, 4)
            tabulate(segments - 1, far, 0, 2)

        @pl.when((j > 0) & (j < far))
        def _():
            tabulate(2 * j - 1, j, 0, 4)
            tabulate(2 * j, j, 1, 4)

        return carry

    lax.fori_loop(0, heads, chain, 0)
    rows_ref[...] = tall[...].astype(jnp.bfloat16).reshape(tok, heads, dim)
    pltpu.make_async_copy(index_ref, idx_ref, index_sem).wait()

    def part(ref, h):
        return ref.at[pl.ds(h * half, half)]

    def climb_copy(source, slot, h):
        return pltpu.make_async_remote_copy(
            src_ref=part(source, h),
            dst_ref=part(climb.at[slot], h),
            send_sem=climb_send.at[slot, h],
            recv_sem=climb_recv.at[slot, h],
            device_id=(above, col),
            device_id_type=MESH,
        )

    def sink_copy(source, slot, h):
        return pltpu.make_async_remote_copy(
            src_ref=part(source, h),
            dst_ref=part(sink.at[slot], h),
            send_sem=sink_send.at[slot, h],
            recv_sem=sink_recv.at[slot, h],
            device_id=(below, col),
            device_id_type=MESH,
        )

    def distant_copy(source, target, h):
        return pltpu.make_async_remote_copy(
            src_ref=part(source, h),
            dst_ref=part(distant, h),
            send_sem=distant_send.at[h],
            recv_sem=distant_recv.at[h],
            device_id=(target, col),
            device_id_type=MESH,
        )

    for h in range(2):
        climb_copy(rows_ref, 1, h).start()
        sink_copy(rows_ref, 1, h).start()
    climb[0] = rows_ref[...]
    sink[0] = rows_ref[...]
    flat[pairs] = jnp.zeros(flat.shape[1:], jnp.bfloat16)
    got_up[0, pl.ds(half, half)] = jnp.zeros((half, mixed_ref.shape[1]), jnp.bfloat16)
    got_down[0, pl.ds(0, half)] = jnp.zeros((half, mixed_ref.shape[1]), jnp.bfloat16)

    def rows_to_wide(rows, count):
        tall[: count * heads, :] = rows.reshape(count * heads, dim).astype(jnp.float32)
        for j in range(heads):
            wide[:count, j * dim : (j + 1) * dim] = tall[
                pl.ds(j, count, stride=heads), :
            ].astype(jnp.bfloat16)

    def send_out(source, target, send_sem, recv_sem, p, i, each):
        other = lax.rem(col + i, columns)
        some = pl.ds(0, each)

        @pl.when(i == 0)
        def _():
            pltpu.make_async_copy(
                source.at[p, col, some], target.at[p, col, some], recv_sem.at[p]
            ).start()

        @pl.when(i > 0)
        def _():
            pltpu.make_async_remote_copy(
                src_ref=source.at[p, other, some],
                dst_ref=target.at[p, col, some],
                send_sem=send_sem.at[p],
                recv_sem=recv_sem.at[p],
                device_id=(seg, other),
                device_id_type=MESH,
            ).start()

    def wait_all(target, sem, p, each):
        piece = target.at[p, :, pl.ds(0, each)]
        pltpu.make_async_copy(piece, piece, sem.at[p]).wait()

    def wait_sent(source, sem, p, each):
        piece = source.at[p, pl.ds(0, columns - 1), pl.ds(0, each)]
        pltpu.make_async_copy(piece, piece, sem.at[p]).wait()

    def dispatch(p, each, slots):
        def one(i, carry):
            other = lax.rem(col + i, columns)
            for r in range(each):
                stage[p, other, r] = pick[r // 2, idx_ref[slots[r // 2], other, r % 2]]
            send_out(stage, arrive, stage_send, arrive_recv, p, i, each)
            return carry

        lax.fori_loop(0, columns, one, 0)

    def experts(p, each):
        count = columns * each
        wait_all(arrive, arrive_recv, p, each)
        wait_sent(stage, stage_send, p, each)
        rows_to_wide(arrive[p, :, :each].reshape(count, heads, dim), count)
        rows = wide[:count, :]
        gate_part = jnp.dot(rows, gate_ref[...], preferred_element_type=jnp.float32)
        up_part = jnp.dot(rows, up_ref[...], preferred_element_type=jnp.float32)
        hidden = (gate_part * jax.nn.sigmoid(gate_part) * up_part).astype(jnp.bfloat16)
        for j in range(heads):
            tall[pl.ds(j, count, stride=heads), :] = jnp.dot(
                hidden,
                down_ref[:, j * dim : (j + 1) * dim],
                preferred_element_type=jnp.float32,
            )
        stage[p, :, :each] = (
            tall[: count * heads, :].astype(jnp.bfloat16).reshape(columns, each, heads, dim)
        )

        def one(i, carry):
            send_out(stage, back, back_send, back_recv, p, i, each)
            return carry

        lax.fori_loop(0, columns, one, 0)

    def land(p, each):
        count = columns * each
        wait_all(back, back_recv, p, each)
        rows_to_wide(back[p, :, :each].reshape(count, heads, dim), count)
        flat[p, pl.ds(0, count)] = wide[:count, :]

    def gather_step(p, carry):
        for h in range(2):
            @pl.when(p >= 1)
            def _():
                climb_copy(rows_ref, p, h).wait_recv()

            @pl.when((p >= 1) & (p < pairs - 1))
            def _():
                climb_copy(climb.at[p], p + 1, h).start()

            @pl.when(p >= 1)
            def _():
                sink_copy(rows_ref, p, h).wait_recv()

            @pl.when((p >= 1) & (p < pairs - 1))
            def _():
                sink_copy(sink.at[p], p + 1, h).start()

            @pl.when(p == pairs - 1)
            def _():
                if h == 0:
                    distant_copy(climb.at[pairs - 1], above, 0).start()
                else:
                    distant_copy(sink.at[pairs - 1], below, 1).start()

        pick[0] = climb[p]
        pick[1] = sink[p]
        dispatch(p, 4, (jnp.maximum(2 * p - 1, 0), 2 * p))

        @pl.when(p == 1)
        def _():
            for k, (source, target) in enumerate(
                ((gate_in, gate_ref), (up_in, up_ref), (down_in, down_ref))
            ):
                load(source, target, k + 4).wait()

        @pl.when(p >= 1)
        def _():
            experts(p - 1, 4)

        @pl.when(p >= 2)
        def _():
            land(p - 2, 4)

        return carry

    lax.fori_loop(0, pairs, gather_step, 0)
    for h in range(2):
        distant_copy(rows_ref, above, h).wait_recv()
    pick[0] = distant[...]
    dispatch(pairs, 2, (segments - 1,))
    experts(pairs - 1, 4)
    land(pairs - 2, 4)
    experts(pairs, 2)
    land(pairs - 1, 4)
    land(pairs, 2)

    def term(p, source, h):
        weights = mix_ref[p, source, pl.ds(h * half, half), :]
        rows = flat[p]
        slots = rows.shape[0]
        return jnp.dot(
            weights[:, :slots], rows, preferred_element_type=jnp.float32
        ) + jnp.dot(weights[:, slots:], rows, preferred_element_type=jnp.float32)

    def up_copy(i, h):
        return pltpu.make_async_remote_copy(
            src_ref=part(sum_up.at[lax.rem(i, 2)], h),
            dst_ref=part(got_up.at[i], h),
            send_sem=up_send.at[i, h],
            recv_sem=up_recv.at[i, h],
            device_id=(above, col),
            device_id_type=MESH,
        )

    def down_copy(i, h):
        return pltpu.make_async_remote_copy(
            src_ref=part(sum_down.at[lax.rem(i, 2)], h),
            dst_ref=part(got_down.at[i], h),
            send_sem=down_send.at[i, h],
            recv_sem=down_recv.at[i, h],
            device_id=(below, col),
            device_id_type=MESH,
        )

    sum_up[0, pl.ds(0, half)] = term(pairs, 0, 0).astype(jnp.bfloat16)
    up_copy(0, 0).start()
    sum_down[0, pl.ds(half, half)] = term(pairs, 0, 1).astype(jnp.bfloat16)
    down_copy(0, 1).start()

    def reduce_step(i, carry):
        for h in range(2):
            spot = pl.ds(h * half, half)
            mine = term(pairs - i, 1, h)

            @pl.when((i > 1) | (h == 0))
            def _():
                up_copy(i - 1, h).wait_recv()


            @pl.when((i > 2) | ((i == 2) & (h == 0)))
            def _():
                up_copy(i - 2, h).wait_send()

            sum_up[lax.rem(i, 2), spot] = (mine + got_up[i - 1, spot].astype(jnp.float32)).astype(
                jnp.bfloat16
            )
            up_copy(i, h).start()
            mine = term(pairs - i, 0, h)

            @pl.when((i > 1) | (h == 1))
            def _():
                down_copy(i - 1, h).wait_recv()


            @pl.when((i > 2) | ((i == 2) & (h == 1)))
            def _():
                down_copy(i - 2, h).wait_send()

            sum_down[lax.rem(i, 2), spot] = (
                mine + got_down[i - 1, spot].astype(jnp.float32)
            ).astype(jnp.bfloat16)
            down_copy(i, h).start()

        return carry

    lax.fori_loop(1, pairs, reduce_step, 0)
    for h in range(2):
        spot = pl.ds(h * half, half)
        total = mixed_ref[spot, :].astype(jnp.float32) + term(0, 0, h)
        up_copy(pairs - 1, h).wait_recv()
        total = total + got_up[pairs - 1, spot].astype(jnp.float32)
        down_copy(pairs - 1, h).wait_recv()
        total = total + got_down[pairs - 1, spot].astype(jnp.float32)
        out_ref[spot, :] = total.astype(jnp.bfloat16)

    def drain(p, carry):
        wait_sent(stage, back_send, p, 4)
        for h in range(2):

            @pl.when(p >= 1)
            def _():
                climb_copy(rows_ref, p, h).wait_send()
                sink_copy(rows_ref, p, h).wait_send()

            @pl.when(p >= pairs - 2)
            def _():
                up_copy(p, h).wait_send()
                down_copy(p, h).wait_send()

        return carry

    lax.fori_loop(0, pairs, drain, 0)
    wait_sent(stage, back_send, pairs, 2)
    for h in range(2):
        distant_copy(rows_ref, above, h).wait_send()
    pltpu.make_async_copy(final_ref, final_ref, final_recv).wait()

    for r in range(cached):
        replaced = jnp.where(slot_ref[0] == r, 1.0, 0.0)
        store_out_ref[r, 0] = (
            final_ref[:, :dim].astype(jnp.float32) * replaced
            + store_ref[r, 0].astype(jnp.float32) * (1.0 - replaced)
        ).astype(jnp.bfloat16)

    def routes_sent(k, carry):
        routes_copy(k, 2 * k - 1).wait_send()
        routes_copy(segments - k, 2 * k).wait_send()
        return carry

    lax.fori_loop(1, far, routes_sent, 0)
    routes_copy(far, segments - 1).wait_send()
    sent = offer.at[pl.ds(0, columns - 1)]
    pltpu.make_async_copy(sent, sent, offer_send).wait()

    @pl.when(seg > 0)
    def _():
        origin_copy().wait_send()

    def drain(j, carry):
        @pl.when(seg < segments - 1)
        def _():
            hand_on(j, 0).wait_send()

        @pl.when((seg == segments - 1) & (j < segments - 1))
        def _():
            end_copy(j).wait_send()

        return carry

    lax.fori_loop(0, heads, drain, 0)


def mixer(lengths, places, slots, beta, decay, gain, ids, weights, store, k, q, v, w_gate, w_up, w_down):
    segments = lax.axis_size("segment")
    columns = lax.axis_size("expert")
    pairs = segments // 2
    heads = segments
    tok, width = v.shape
    dim = store.shape[-1]
    top = ids.shape[0]
    bf, f32 = jnp.bfloat16, jnp.float32
    dma = pltpu.SemaphoreType.DMA
    whole = pl.BlockSpec(memory_space=pltpu.VMEM)
    scalars = pl.BlockSpec(memory_space=pltpu.SMEM)
    remote = pl.BlockSpec(memory_space=pl.ANY)
    return pl.pallas_call(
        mixer_kernel,
        out_shape=(
            jax.ShapeDtypeStruct((tok, width), bf),
            jax.ShapeDtypeStruct(store.shape, bf),
        ),
        in_specs=[scalars] * 3 + [whole] * 5 + [remote] * 7,
        out_specs=(whole, whole),
        scratch_shapes=[
            pltpu.VMEM(store.shape, bf),
            pltpu.VMEM(k.shape, bf),
            pltpu.VMEM(q.shape, bf),
            pltpu.VMEM(v.shape, bf),
            pltpu.VMEM(w_gate.shape, bf),
            pltpu.VMEM(w_up.shape, bf),
            pltpu.VMEM(w_down.shape, bf),
            pltpu.VMEM((2 * top, tok), f32),
            pltpu.VMEM((segments, 2 * top, tok), f32),
            pltpu.VMEM((segments, columns, tok), jnp.int32),
            pltpu.SMEM((segments, columns, tok), jnp.int32),
            pltpu.VMEM((pairs + 1, 2, tok, 2 * tok), bf),
            pltpu.VMEM((tok, tok), f32),
            pltpu.VMEM((tok, width), bf),
            pltpu.VMEM((tok, heads, dim), bf),
            pltpu.VMEM((dim, 2 * dim), bf),
            pltpu.VMEM((columns, dim, dim), bf),
            pltpu.VMEM((columns, dim, dim), bf),
            pltpu.VMEM((dim, 2 * dim), bf),
            pltpu.VMEM((heads, dim, 2 * dim), bf),
            pltpu.VMEM((heads, dim, 2 * dim), bf),
            pltpu.VMEM((heads, 2 * dim, 2 * dim), bf),
            pltpu.VMEM((heads, 2 * dim, dim), f32),
            pltpu.VMEM((tok, heads), f32),
            pltpu.VMEM((tok, heads), f32),
            pltpu.VMEM((heads, tok), f32),
            pltpu.VMEM((pairs, tok, heads, dim), bf),
            pltpu.VMEM((pairs, tok, heads, dim), bf),
            pltpu.VMEM((tok, heads, dim), bf),
            pltpu.VMEM((2, tok, heads, dim), bf),
            pltpu.VMEM((pairs + 1, columns, 4, heads, dim), bf),
            pltpu.VMEM((pairs + 1, columns, 4, heads, dim), bf),
            pltpu.VMEM((pairs + 1, columns, 4, heads, dim), bf),
            pltpu.VMEM((pairs + 1, columns * 4, width), bf),
            pltpu.VMEM((2, tok, width), bf),
            pltpu.VMEM((2, tok, width), bf),
            pltpu.VMEM((pairs, tok, width), bf),
            pltpu.VMEM((pairs, tok, width), bf),
            pltpu.VMEM((tok * heads, dim), f32),
            pltpu.VMEM((tok, width), bf),
            dma((7,)),
            dma((segments,)),
            dma,
            dma,
            dma,
            dma,
            dma,
            dma((heads,)),
            dma((heads,)),
            dma((heads,)),
            dma,
            dma((2,)),
            dma((2,)),
            dma((pairs, 2)),
            dma((pairs, 2)),
            dma((pairs, 2)),
            dma((pairs, 2)),
            dma((pairs + 1,)),
            dma((pairs + 1,)),
            dma((pairs + 1,)),
            dma((pairs + 1,)),
            dma((pairs, 2)),
            dma((pairs, 2)),
            dma((pairs, 2)),
            dma((pairs, 2)),
        ],
        compiler_params=pltpu.CompilerParams(
            collective_id=1, has_side_effects=True, vmem_limit_bytes=62 * 1024 * 1024
        ),
    )(lengths, places, slots, beta, decay, gain, ids, weights, store, k, q, v, w_gate, w_up, w_down)


def shards(
    q_heads,
    k_heads,
    values,
    beta,
    decay,
    head_gain,
    suffix_len,
    store_states,
    cache_row,
    write_slot,
    expert_ids,
    route_weight,
    w_gate,
    w_up,
    w_down,
):
    out, store_out = mixer(
        suffix_len,
        cache_row,
        write_slot,
        beta[0].T,
        decay[0].T,
        head_gain.reshape(1, -1),
        expert_ids[0].T,
        route_weight[0].T,
        store_states,
        k_heads[0],
        q_heads[0],
        values[0],
        w_gate[0],
        w_up[0],
        w_down[0],
    )
    return (out[None], store_out)


def solution(mesh):
    return jax.shard_map(
        shards,
        mesh=mesh,
        in_specs=(
            P("expert", "segment", None),
            P("expert", "segment", None),
            P("expert", "segment", None),
            P("expert", "segment", None),
            P("expert", "segment", None),
            P(),
            P("expert"),
            P("expert", "segment", None, None),
            P(),
            P("expert"),
            P("expert", "segment", None),
            P("expert", "segment", None),
            P(("segment", "expert"), None, None),
            P(("segment", "expert"), None, None),
            P(("segment", "expert"), None, None),
        ),
        out_specs=(P("expert", "segment", None), P("expert", "segment", None, None)),
        check_vma=False,
    )
```

```python
import jax
import jax.numpy as jnp
from jax import lax
from jax.experimental import pallas as pl
from jax.experimental.pallas import tpu as pltpu
from jax.sharding import PartitionSpec as P

MESH = pl.DeviceIdType.MESH


GROUP = 4
UNROLL = 5
PARTS = 4


def halves(block):
    high = block.astype(jnp.bfloat16)
    low = (block - high.astype(jnp.float32)).astype(jnp.bfloat16)
    return high, low


def left_pair(block):
    high, low = halves(block)
    return jnp.concatenate([high, low], axis=1)


def right_pair(block):
    high, low = halves(block)
    row = jnp.concatenate([high, low], axis=1)
    return jnp.concatenate([row, row], axis=0)


def paired_dot(left, right):
    both = jnp.dot(left, right, preferred_element_type=jnp.float32)
    width = both.shape[1] // 2
    return both[:, :width] + both[:, width:]


def unit_rows(block, factor):
    squares = jnp.sum(block * block, axis=-1, keepdims=True)
    return block * (lax.rsqrt(squares + 1e-06) * factor)


def mixer_kernel(
    len_ref,
    row_ref,
    slot_ref,
    beta_ref,
    decay_ref,
    gain_ref,
    ids_ref,
    weight_ref,
    store_in,
    k_in,
    q_in,
    v_in,
    gate_in,
    up_in,
    down_in,
    out_ref,
    store_out_ref,
    store_ref,
    k_ref,
    q_ref,
    v_ref,
    gate_ref,
    up_ref,
    down_ref,
    routes_ref,
    routes_all,
    index_ref,
    idx_ref,
    mix_ref,
    mixed_ref,
    rows_ref,
    final_ref,
    offer,
    taken,
    origin,
    held,
    passed,
    step_right,
    step_read,
    step_add,
    strength_ref,
    total_ref,
    across_ref,
    climb,
    sink,
    distant,
    pick,
    stage,
    arrive,
    back,
    flat,
    sum_up,
    sum_down,
    got_up,
    got_down,
    tall,
    wide,
    load_sem,
    routes_send,
    routes_recv,
    index_sem,
    offer_send,
    taken_recv,
    origin_send,
    held_recv,
    passed_send,
    ends_send,
    final_recv,
    distant_send,
    distant_recv,
    climb_send,
    climb_recv,
    sink_send,
    sink_recv,
    stage_send,
    arrive_recv,
    back_send,
    back_recv,
    up_send,
    up_recv,
    down_send,
    down_recv,
):
    segments = lax.axis_size("segment")
    columns = lax.axis_size("expert")
    seg = lax.axis_index("segment")
    col = lax.axis_index("expert")
    pairs = segments // 2
    tok = q_ref.shape[0]
    half = tok // 2
    dim = store_ref.shape[-1]
    cached = store_ref.shape[0]
    heads = segments
    share = v_ref.shape[1] // q_ref.shape[1]
    top = ids_ref.shape[0]
    above = lax.rem(seg + 1, segments)
    below = lax.rem(seg + segments - 1, segments)

    def load(source, target, k):
        return pltpu.make_async_copy(source, target, load_sem.at[k])

    for k, (source, target) in enumerate(
        (
            (store_in, store_ref),
            (k_in, k_ref),
            (q_in, q_ref),
            (v_in, v_ref),
            (gate_in, gate_ref),
            (up_in, up_ref),
            (down_in, down_ref),
        )
    ):
        load(source, target, k).start()
    routes_ref[:top] = ids_ref[...].astype(jnp.float32)
    routes_ref[top:] = weight_ref[...]

    barrier = pltpu.get_barrier_semaphore()

    def greet_row(step, carry):
        other = lax.rem(col + step, columns)
        pl.semaphore_signal(barrier, inc=1, device_id=(seg, other), device_id_type=MESH)
        return carry

    def greet_line(step, carry):
        other = lax.rem(seg + step, segments)
        pl.semaphore_signal(barrier, inc=1, device_id=(other, col), device_id_type=MESH)
        return carry

    lax.fori_loop(1, columns, greet_row, 0)
    lax.fori_loop(1, segments, greet_line, 0)
    pl.semaphore_wait(barrier, columns + segments - 2)

    far = segments // 2
    pltpu.make_async_copy(routes_ref, routes_all.at[0], routes_recv).start()

    def routes_copy(step, slot):
        return pltpu.make_async_remote_copy(
            src_ref=routes_ref,
            dst_ref=routes_all.at[slot],
            send_sem=routes_send.at[slot],
            recv_sem=routes_recv,
            device_id=(lax.rem(seg + step, segments), col),
            device_id_type=MESH,
        )

    def routes_out(k, carry):
        routes_copy(k, 2 * k - 1).start()
        routes_copy(segments - k, 2 * k).start()
        return carry

    lax.fori_loop(1, far, routes_out, 0)
    routes_copy(far, segments - 1).start()

    @pl.when(seg == 0)
    def _():
        held[:, :, dim:] = jnp.zeros((heads, dim, dim), jnp.bfloat16)

    load(store_in, store_ref, 0).wait()

    def propose(i, carry):
        other = lax.rem(col + i, columns)
        wanted = row_ref[other]
        block = jnp.zeros((dim, dim), jnp.bfloat16)
        for r in range(cached):
            match = jnp.where(wanted == col * cached + r, 1.0, 0.0)
            match = jnp.full((dim, dim), match, jnp.float32).astype(jnp.bfloat16)
            block = block + store_ref[r, 0] * match
        offer[other] = block

        @pl.when(i == 0)
        def _():
            pltpu.make_async_copy(offer.at[col], taken.at[col], taken_recv).start()

        @pl.when(i > 0)
        def _():
            pltpu.make_async_remote_copy(
                src_ref=offer.at[other],
                dst_ref=taken.at[col],
                send_sem=offer_send,
                recv_sem=taken_recv,
                device_id=(seg, other),
                device_id_type=MESH,
            ).start()

        return carry

    lax.fori_loop(0, columns, propose, 0)

    line = lax.broadcasted_iota(jnp.int32, (tok, tok), 0)
    lane = lax.broadcasted_iota(jnp.int32, (tok, tok), 1)
    place = lax.broadcasted_iota(jnp.int32, (tok, 1), 0)
    valid = jnp.where(place + seg * tok < len_ref[0], 1.0, 0.0)
    along = lax.broadcasted_iota(jnp.int32, (1, tok), 1)
    valid_along = jnp.where(along + seg * tok < len_ref[0], 1.0, 0.0)
    logs = (decay_ref[...].astype(jnp.float32) * valid_along).astype(jnp.bfloat16)
    writes = (beta_ref[...].astype(jnp.float32) * valid_along).astype(jnp.bfloat16)
    lower = jnp.where(line >= lane, 1.0, 0.0).astype(jnp.bfloat16)
    upper = jnp.where(line <= lane, 1.0, 0.0).astype(jnp.bfloat16)
    diagonal = jnp.where(line == lane, 1.0, 0.0).astype(jnp.bfloat16)
    turned = (((1,), (1,)), ((), ()))
    across_ref[...] = jnp.dot(logs, upper, preferred_element_type=jnp.float32)
    total_ref[...] = lax.dot_general(lower, logs, turned, preferred_element_type=jnp.float32)
    strength_ref[...] = lax.dot_general(
        diagonal, writes, turned, preferred_element_type=jnp.float32
    )
    for k, (source, target) in enumerate(((k_in, k_ref), (q_in, q_ref), (v_in, v_ref))):
        load(source, target, k + 1).wait()
    identity = jnp.where(line == lane, 1.0, 0.0)
    which = lax.broadcasted_iota(jnp.int32, (tok, heads), 1)

    def column_of(ref, j):
        return jnp.sum(jnp.where(which == j, ref[...], 0.0), axis=1, keepdims=True)

    def local_work(i, carry):
        grams, across_keys, unit_keys, unit_queries = [], [], [], []
        for g in range(GROUP):
            spot = pl.ds(pl.multiple_of((i * GROUP + g) * dim, dim), dim)
            keys = unit_rows(k_ref[:, spot].astype(jnp.float32), 1.0)
            queries = unit_rows(q_ref[:, spot].astype(jnp.float32), dim ** (-0.5))
            unit_keys.append(keys)
            unit_queries.append(queries)
            across_keys.append(keys.T)
        for g in range(GROUP):
            grams.append(
                paired_dot(
                    left_pair(jnp.concatenate([unit_keys[g], unit_queries[g]], axis=0)),
                    right_pair(across_keys[g]),
                )
            )
        count = GROUP * share
        number = [i * count + a for a in range(count)]
        strength = [column_of(strength_ref, j) for j in number]
        total = [column_of(total_ref, j) for j in number]
        across = [across_ref[pl.ds(j, 1), :] for j in number]
        upto = [
            jnp.where(line >= lane, jnp.exp(jnp.where(line >= lane, total[a] - across[a], 0.0)), 0.0)
            for a in range(count)
        ]
        coupling = [
            jnp.where(line > lane, strength[a] * upto[a] * grams[a // share][:tok], 0.0)
            for a in range(count)
        ]
        inverse = [
            identity - jnp.where((line == lane + 1) & (line % 2 == 1), coupling[a], 0.0)
            for a in range(count)
        ]
        size = 2
        while size < tok:
            corner = (
                (line // (2 * size) == lane // (2 * size))
                & ((line // size) % 2 == 1)
                & ((lane // size) % 2 == 0)
            )
            inner = [
                paired_dot(
                    left_pair(jnp.where(corner, coupling[a], 0.0)), right_pair(inverse[a])
                )
                for a in range(count)
            ]
            inverse = [
                inverse[a] - paired_dot(left_pair(inverse[a]), right_pair(inner[a]))
                for a in range(count)
            ]
            size *= 2
        growth = [jnp.exp(total[a]) for a in range(count)]
        solver = [left_pair(inverse[a]) for a in range(count)]
        pseudo = []
        for a in range(count):
            spot = pl.ds(pl.multiple_of(number[a] * dim, dim), dim)
            values = v_ref[:, spot].astype(jnp.float32)
            pseudo.append(right_pair(paired_dot(solver[a], right_pair(strength[a] * values))))
        weights = [
            right_pair(
                paired_dot(solver[a], right_pair((strength[a] * growth[a]) * unit_keys[a // share]))
            )
            for a in range(count)
        ]
        for a in range(count):
            last = across[a][:, tok - 1 :]
            tail = across_keys[a // share] * jnp.exp(last - across[a])
            scores = upto[a] * grams[a // share][tok:]
            left = left_pair(jnp.concatenate([tail, scores], axis=0))
            minus = paired_dot(left, weights[a])
            plus = paired_dot(left, pseudo[a])
            step_right[number[a]] = right_pair((jnp.exp(last) * identity - minus[:dim]).T)
            step_add[number[a], :dim] = plus[:dim].T
            step_add[number[a], dim:] = plus[dim:]
            high, low = halves(growth[a] * unit_queries[a // share] - minus[dim:])
            read = jnp.concatenate([high, low], axis=0)
            step_read[number[a]] = jnp.concatenate([read, read], axis=1)
        return carry

    rows_each = dim // PARTS

    def hand_on(j, h):
        some = pl.ds(h * rows_each, rows_each)
        return pltpu.make_async_remote_copy(
            src_ref=passed.at[j, some],
            dst_ref=held.at[j, some],
            send_sem=passed_send.at[j, h],
            recv_sem=held_recv.at[j, h],
            device_id=(seg + 1, col),
            device_id_type=MESH,
        )

    def origin_copy():
        return pltpu.make_async_remote_copy(
            src_ref=origin,
            dst_ref=held.at[seg, :, pl.ds(0, dim)],
            send_sem=origin_send,
            recv_sem=held_recv.at[seg, 0],
            device_id=(0, col),
            device_id_type=MESH,
        )

    def end_copy(j):
        return pltpu.make_async_remote_copy(
            src_ref=passed.at[j],
            dst_ref=final_ref,
            send_sem=ends_send.at[j],
            recv_sem=final_recv,
            device_id=(j, col),
            device_id_type=MESH,
        )

    def give_origin():
        pltpu.make_async_copy(taken, taken, taken_recv).wait()

        def add_up(i, block):
            return block + taken[i].astype(jnp.float32)

        block = lax.fori_loop(0, columns, add_up, jnp.zeros((dim, dim), jnp.float32))
        origin[...] = block.T.astype(jnp.bfloat16)

        @pl.when(seg == 0)
        def _():
            pltpu.make_async_copy(origin, held.at[0, :, pl.ds(0, dim)], held_recv.at[0, 0]).start()

        @pl.when(seg > 0)
        def _():
            origin_copy().start()

    lax.fori_loop(0, heads // share // GROUP, local_work, 0)

    names = lax.broadcasted_iota(jnp.int32, (columns, 1), 0) + seg * columns
    token = lax.broadcasted_iota(jnp.int32, (columns, tok), 1)

    def locate(slot):
        routes = routes_all[slot]
        top = routes.shape[0] // 2
        weight = jnp.zeros((columns, tok), jnp.float32)
        first = jnp.full((columns, tok), tok, jnp.int32)
        last = jnp.full((columns, tok), -1, jnp.int32)
        for k in range(top):
            same = routes[k : k + 1, :].astype(jnp.int32) == names
            weight = weight + jnp.where(same, routes[top + k : top + k + 1, :], 0.0)
            first = jnp.where(same, token, first)
            last = jnp.where(same, token, last)
        first = jnp.min(first, axis=1, keepdims=True)
        last = jnp.max(last, axis=1, keepdims=True)
        index_ref[slot] = jnp.where(token == 0, jnp.where(first < tok, first, 0), jnp.maximum(last, 0))
        pltpu.make_async_copy(index_ref.at[slot], idx_ref.at[slot], index_sem).start()
        at_first = jnp.where(token == first, weight, 0.0)
        at_last = jnp.where((token == last) & (last != first), weight, 0.0)
        return at_first, at_last

    def tabulate(slot, p, source, width):
        at_first, at_last = locate(slot)
        tall[:tok] = jnp.zeros((tok, tok), jnp.float32)
        tall[pl.ds(2 * source, columns, stride=width), :] = at_first
        tall[pl.ds(2 * source + 1, columns, stride=width), :] = at_last
        mix_ref[p, source] = left_pair(tall[:tok].T)

    def chain(j, carry):
        for h in range(PARTS):
            some = pl.ds(h * rows_each, rows_each)
            if h == 0:

                @pl.when(seg == 0)
                def _():
                    piece = held.at[j, :, pl.ds(0, dim)]
                    pltpu.make_async_copy(piece, piece, held_recv.at[j, 0]).wait()

            @pl.when(seg > 0)
            def _():
                piece = held.at[j, some]
                pltpu.make_async_copy(piece, piece, held_recv.at[j, h]).wait()

            passed[j, some] = left_pair(
                paired_dot(held[j, some], step_right[j]) + step_add[j, some]
            )

            @pl.when(seg < segments - 1)
            def _():
                hand_on(j, h).start()

        @pl.when((seg == segments - 1) & (j < segments - 1))
        def _():
            end_copy(j).start()

        @pl.when((seg == segments - 1) & (j == segments - 1))
        def _():
            pltpu.make_async_copy(passed.at[j], final_ref, final_recv).start()

        both = lax.dot_general(
            step_read[j], held[j], turned, preferred_element_type=jnp.float32
        )
        raw = (both[:tok] + both[tok:] + step_add[j, dim:]) * valid
        squares = jnp.sum(raw * raw, axis=-1, keepdims=True) * (1.0 / dim)
        normed = raw * lax.rsqrt(squares + 1e-06) * gain_ref[...]
        mixed_ref[:, pl.ds(pl.multiple_of(j * dim, dim), dim)] = normed.astype(jnp.bfloat16)
        tall[pl.ds(j, tok, stride=heads), :] = normed
        return carry

    def tables(k, carry):
        tabulate(2 * k - 1, k, 0, 4)
        tabulate(2 * k, k, 1, 4)
        return carry

    pltpu.make_async_copy(routes_all, routes_all, routes_recv).wait()
    tabulate(0, 0, 0, 4)
    tabulate(segments - 1, far, 0, 2)
    give_origin()
    lax.fori_loop(1, far, tables, 0)
    lax.fori_loop(0, heads, chain, 0)
    rows_ref[...] = tall[...].astype(jnp.bfloat16).reshape(tok, heads, dim)
    pltpu.make_async_copy(index_ref, idx_ref, index_sem).wait()

    def part(ref, h):
        return ref.at[pl.ds(h * half, half)]

    def climb_copy(source, slot, h):
        return pltpu.make_async_remote_copy(
            src_ref=part(source, h),
            dst_ref=part(climb.at[slot], h),
            send_sem=climb_send.at[slot, h],
            recv_sem=climb_recv.at[slot, h],
            device_id=(above, col),
            device_id_type=MESH,
        )

    def sink_copy(source, slot, h):
        return pltpu.make_async_remote_copy(
            src_ref=part(source, h),
            dst_ref=part(sink.at[slot], h),
            send_sem=sink_send.at[slot, h],
            recv_sem=sink_recv.at[slot, h],
            device_id=(below, col),
            device_id_type=MESH,
        )

    def distant_copy(source, target, h):
        return pltpu.make_async_remote_copy(
            src_ref=part(source, h),
            dst_ref=part(distant, h),
            send_sem=distant_send.at[h],
            recv_sem=distant_recv.at[h],
            device_id=(target, col),
            device_id_type=MESH,
        )

    for h in range(2):
        climb_copy(rows_ref, 1, h).start()
        sink_copy(rows_ref, 1, h).start()
    climb[0] = rows_ref[...]
    sink[0] = rows_ref[...]
    flat[pairs] = jnp.zeros(flat.shape[1:], jnp.bfloat16)
    got_up[0, pl.ds(half, half)] = jnp.zeros((half, mixed_ref.shape[1]), jnp.bfloat16)
    got_down[0, pl.ds(0, half)] = jnp.zeros((half, mixed_ref.shape[1]), jnp.bfloat16)

    def rows_to_wide(rows, count):
        tall[: count * heads, :] = rows.reshape(count * heads, dim).astype(jnp.float32)
        for j in range(heads):
            wide[:count, j * dim : (j + 1) * dim] = tall[
                pl.ds(j, count, stride=heads), :
            ].astype(jnp.bfloat16)

    def to_all(step):
        def some_of(i, carry):
            for u in range(UNROLL):
                step(1 + i * UNROLL + u)
            return carry

        rounds = (columns - 1) // UNROLL
        lax.fori_loop(0, rounds, some_of, 0)
        for rest in range(1 + rounds * UNROLL, columns):
            step(rest)

    def keep_own(source, target, recv_sem, p, each):
        some = pl.ds(0, each)
        pltpu.make_async_copy(
            source.at[p, col, some], target.at[p, col, some], recv_sem.at[p]
        ).start()

    def send_out(source, target, send_sem, recv_sem, p, other, each):
        some = pl.ds(0, each)
        pltpu.make_async_remote_copy(
            src_ref=source.at[p, other, some],
            dst_ref=target.at[p, col, some],
            send_sem=send_sem.at[p],
            recv_sem=recv_sem.at[p],
            device_id=(seg, other),
            device_id_type=MESH,
        ).start()

    def wait_all(target, sem, p, each):
        piece = target.at[p, :, pl.ds(0, each)]
        pltpu.make_async_copy(piece, piece, sem.at[p]).wait()

    def wait_sent(source, sem, p, each):
        piece = source.at[p, pl.ds(0, columns - 1), pl.ds(0, each)]
        pltpu.make_async_copy(piece, piece, sem.at[p]).wait()

    def dispatch(p, each, slots):
        def choose(other):
            for r in range(each):
                stage[p, other, r] = pick[r // 2, idx_ref[slots[r // 2], other, r % 2]]

        def step(i):
            other = lax.rem(col + i, columns)
            choose(other)
            send_out(stage, arrive, stage_send, arrive_recv, p, other, each)

        to_all(step)
        choose(col)
        keep_own(stage, arrive, arrive_recv, p, each)

    def experts(p, each):
        count = columns * each
        wait_all(arrive, arrive_recv, p, each)
        wait_sent(stage, stage_send, p, each)
        rows_to_wide(arrive[p, :, :each].reshape(count, heads, dim), count)
        rows = wide[:count, :]
        gate_part = jnp.dot(rows, gate_ref[...], preferred_element_type=jnp.float32)
        up_part = jnp.dot(rows, up_ref[...], preferred_element_type=jnp.float32)
        hidden = (gate_part * jax.nn.sigmoid(gate_part) * up_part).astype(jnp.bfloat16)
        for j in range(heads):
            tall[pl.ds(j, count, stride=heads), :] = jnp.dot(
                hidden,
                down_ref[:, j * dim : (j + 1) * dim],
                preferred_element_type=jnp.float32,
            )
        stage[p, :, :each] = (
            tall[: count * heads, :].astype(jnp.bfloat16).reshape(columns, each, heads, dim)
        )

        def step(i):
            send_out(stage, back, back_send, back_recv, p, lax.rem(col + i, columns), each)

        to_all(step)
        keep_own(stage, back, back_recv, p, each)

    def land(p, each):
        count = columns * each
        wait_all(back, back_recv, p, each)
        rows_to_wide(back[p, :, :each].reshape(count, heads, dim), count)
        flat[p, pl.ds(0, count)] = wide[:count, :]

    def gather_step(p, carry):
        for h in range(2):
            @pl.when(p >= 1)
            def _():
                climb_copy(rows_ref, p, h).wait_recv()

            @pl.when((p >= 1) & (p < pairs - 1))
            def _():
                climb_copy(climb.at[p], p + 1, h).start()

            @pl.when(p >= 1)
            def _():
                sink_copy(rows_ref, p, h).wait_recv()

            @pl.when((p >= 1) & (p < pairs - 1))
            def _():
                sink_copy(sink.at[p], p + 1, h).start()

            @pl.when(p == pairs - 1)
            def _():
                if h == 0:
                    distant_copy(climb.at[pairs - 1], above, 0).start()
                else:
                    distant_copy(sink.at[pairs - 1], below, 1).start()

        pick[0] = climb[p]
        pick[1] = sink[p]
        dispatch(p, 4, (jnp.maximum(2 * p - 1, 0), 2 * p))

        @pl.when(p == 1)
        def _():
            for k, (source, target) in enumerate(
                ((gate_in, gate_ref), (up_in, up_ref), (down_in, down_ref))
            ):
                load(source, target, k + 4).wait()

        @pl.when(p >= 1)
        def _():
            experts(p - 1, 4)

        @pl.when(p >= 2)
        def _():
            land(p - 2, 4)

        return carry

    lax.fori_loop(0, pairs, gather_step, 0)
    for h in range(2):
        distant_copy(rows_ref, above, h).wait_recv()
    pick[0] = distant[...]
    dispatch(pairs, 2, (segments - 1,))
    experts(pairs - 1, 4)
    land(pairs - 2, 4)
    experts(pairs, 2)
    land(pairs - 1, 4)
    land(pairs, 2)

    def term(p, source, h):
        weights = mix_ref[p, source, pl.ds(h * half, half), :]
        rows = flat[p]
        slots = rows.shape[0]
        return jnp.dot(
            weights[:, :slots], rows, preferred_element_type=jnp.float32
        ) + jnp.dot(weights[:, slots:], rows, preferred_element_type=jnp.float32)

    def up_copy(i, h):
        return pltpu.make_async_remote_copy(
            src_ref=part(sum_up.at[lax.rem(i, 2)], h),
            dst_ref=part(got_up.at[i], h),
            send_sem=up_send.at[i, h],
            recv_sem=up_recv.at[i, h],
            device_id=(above, col),
            device_id_type=MESH,
        )

    def down_copy(i, h):
        return pltpu.make_async_remote_copy(
            src_ref=part(sum_down.at[lax.rem(i, 2)], h),
            dst_ref=part(got_down.at[i], h),
            send_sem=down_send.at[i, h],
            recv_sem=down_recv.at[i, h],
            device_id=(below, col),
            device_id_type=MESH,
        )

    sum_up[0, pl.ds(0, half)] = term(pairs, 0, 0).astype(jnp.bfloat16)
    up_copy(0, 0).start()
    sum_down[0, pl.ds(half, half)] = term(pairs, 0, 1).astype(jnp.bfloat16)
    down_copy(0, 1).start()

    def reduce_step(i, carry):
        for h in range(2):
            spot = pl.ds(h * half, half)
            mine = term(pairs - i, 1, h)

            @pl.when((i > 1) | (h == 0))
            def _():
                up_copy(i - 1, h).wait_recv()


            @pl.when((i > 2) | ((i == 2) & (h == 0)))
            def _():
                up_copy(i - 2, h).wait_send()

            sum_up[lax.rem(i, 2), spot] = (mine + got_up[i - 1, spot].astype(jnp.float32)).astype(
                jnp.bfloat16
            )
            up_copy(i, h).start()
            mine = term(pairs - i, 0, h)

            @pl.when((i > 1) | (h == 1))
            def _():
                down_copy(i - 1, h).wait_recv()


            @pl.when((i > 2) | ((i == 2) & (h == 1)))
            def _():
                down_copy(i - 2, h).wait_send()

            sum_down[lax.rem(i, 2), spot] = (
                mine + got_down[i - 1, spot].astype(jnp.float32)
            ).astype(jnp.bfloat16)
            down_copy(i, h).start()

        return carry

    lax.fori_loop(1, pairs, reduce_step, 0)
    for h in range(2):
        spot = pl.ds(h * half, half)
        total = mixed_ref[spot, :].astype(jnp.float32) + term(0, 0, h)
        up_copy(pairs - 1, h).wait_recv()
        total = total + got_up[pairs - 1, spot].astype(jnp.float32)
        down_copy(pairs - 1, h).wait_recv()
        total = total + got_down[pairs - 1, spot].astype(jnp.float32)
        out_ref[spot, :] = total.astype(jnp.bfloat16)

    def drain(p, carry):
        wait_sent(stage, back_send, p, 4)
        for h in range(2):

            @pl.when(p >= 1)
            def _():
                climb_copy(rows_ref, p, h).wait_send()
                sink_copy(rows_ref, p, h).wait_send()

            @pl.when(p >= pairs - 2)
            def _():
                up_copy(p, h).wait_send()
                down_copy(p, h).wait_send()

        return carry

    lax.fori_loop(0, pairs, drain, 0)
    wait_sent(stage, back_send, pairs, 2)
    for h in range(2):
        distant_copy(rows_ref, above, h).wait_send()
    pltpu.make_async_copy(final_ref, final_ref, final_recv).wait()

    checkpoint = final_ref[:, :dim].astype(jnp.float32).T
    for r in range(cached):
        replaced = jnp.where(slot_ref[0] == r, 1.0, 0.0)
        store_out_ref[r, 0] = (
            checkpoint * replaced
            + store_ref[r, 0].astype(jnp.float32) * (1.0 - replaced)
        ).astype(jnp.bfloat16)

    def routes_sent(k, carry):
        routes_copy(k, 2 * k - 1).wait_send()
        routes_copy(segments - k, 2 * k).wait_send()
        return carry

    lax.fori_loop(1, far, routes_sent, 0)
    routes_copy(far, segments - 1).wait_send()
    sent = offer.at[pl.ds(0, columns - 1)]
    pltpu.make_async_copy(sent, sent, offer_send).wait()

    @pl.when(seg > 0)
    def _():
        origin_copy().wait_send()

    def drain(j, carry):
        @pl.when(seg < segments - 1)
        def _():
            for h in range(PARTS):
                hand_on(j, h).wait_send()

        @pl.when((seg == segments - 1) & (j < segments - 1))
        def _():
            end_copy(j).wait_send()

        return carry

    lax.fori_loop(0, heads, drain, 0)


def mixer(lengths, places, slots, beta, decay, gain, ids, weights, store, k, q, v, w_gate, w_up, w_down):
    segments = lax.axis_size("segment")
    columns = lax.axis_size("expert")
    pairs = segments // 2
    heads = segments
    tok, width = v.shape
    dim = store.shape[-1]
    top = ids.shape[0]
    bf, f32 = jnp.bfloat16, jnp.float32
    dma = pltpu.SemaphoreType.DMA
    whole = pl.BlockSpec(memory_space=pltpu.VMEM)
    scalars = pl.BlockSpec(memory_space=pltpu.SMEM)
    remote = pl.BlockSpec(memory_space=pl.ANY)
    return pl.pallas_call(
        mixer_kernel,
        out_shape=(
            jax.ShapeDtypeStruct((tok, width), bf),
            jax.ShapeDtypeStruct(store.shape, bf),
        ),
        in_specs=[scalars] * 3 + [whole] * 5 + [remote] * 7,
        out_specs=(whole, whole),
        scratch_shapes=[
            pltpu.VMEM(store.shape, bf),
            pltpu.VMEM(k.shape, bf),
            pltpu.VMEM(q.shape, bf),
            pltpu.VMEM(v.shape, bf),
            pltpu.VMEM(w_gate.shape, bf),
            pltpu.VMEM(w_up.shape, bf),
            pltpu.VMEM(w_down.shape, bf),
            pltpu.VMEM((2 * top, tok), f32),
            pltpu.VMEM((segments, 2 * top, tok), f32),
            pltpu.VMEM((segments, columns, tok), jnp.int32),
            pltpu.SMEM((segments, columns, tok), jnp.int32),
            pltpu.VMEM((pairs + 1, 2, tok, 2 * tok), bf),
            pltpu.VMEM((tok, width), bf),
            pltpu.VMEM((tok, heads, dim), bf),
            pltpu.VMEM((dim, 2 * dim), bf),
            pltpu.VMEM((columns, dim, dim), bf),
            pltpu.VMEM((columns, dim, dim), bf),
            pltpu.VMEM((dim, dim), bf),
            pltpu.VMEM((heads, dim, 2 * dim), bf),
            pltpu.VMEM((heads, dim, 2 * dim), bf),
            pltpu.VMEM((heads, 2 * dim, 2 * dim), bf),
            pltpu.VMEM((heads, 2 * dim, 2 * dim), bf),
            pltpu.VMEM((heads, 2 * dim, dim), f32),
            pltpu.VMEM((tok, heads), f32),
            pltpu.VMEM((tok, heads), f32),
            pltpu.VMEM((heads, tok), f32),
            pltpu.VMEM((pairs, tok, heads, dim), bf),
            pltpu.VMEM((pairs, tok, heads, dim), bf),
            pltpu.VMEM((tok, heads, dim), bf),
            pltpu.VMEM((2, tok, heads, dim), bf),
            pltpu.VMEM((pairs + 1, columns, 4, heads, dim), bf),
            pltpu.VMEM((pairs + 1, columns, 4, heads, dim), bf),
            pltpu.VMEM((pairs + 1, columns, 4, heads, dim), bf),
            pltpu.VMEM((pairs + 1, columns * 4, width), bf),
            pltpu.VMEM((2, tok, width), bf),
            pltpu.VMEM((2, tok, width), bf),
            pltpu.VMEM((pairs, tok, width), bf),
            pltpu.VMEM((pairs, tok, width), bf),
            pltpu.VMEM((tok * heads, dim), f32),
            pltpu.VMEM((tok, width), bf),
            dma((7,)),
            dma((segments,)),
            dma,
            dma,
            dma,
            dma,
            dma,
            dma((heads, PARTS)),
            dma((heads, PARTS)),
            dma((heads,)),
            dma,
            dma((2,)),
            dma((2,)),
            dma((pairs, 2)),
            dma((pairs, 2)),
            dma((pairs, 2)),
            dma((pairs, 2)),
            dma((pairs + 1,)),
            dma((pairs + 1,)),
            dma((pairs + 1,)),
            dma((pairs + 1,)),
            dma((pairs, 2)),
            dma((pairs, 2)),
            dma((pairs, 2)),
            dma((pairs, 2)),
        ],
        compiler_params=pltpu.CompilerParams(
            collective_id=1, has_side_effects=True, vmem_limit_bytes=62 * 1024 * 1024
        ),
    )(lengths, places, slots, beta, decay, gain, ids, weights, store, k, q, v, w_gate, w_up, w_down)


def shards(
    q_heads,
    k_heads,
    values,
    beta,
    decay,
    head_gain,
    suffix_len,
    store_states,
    cache_row,
    write_slot,
    expert_ids,
    route_weight,
    w_gate,
    w_up,
    w_down,
):
    out, store_out = mixer(
        suffix_len,
        cache_row,
        write_slot,
        beta[0].T,
        decay[0].T,
        head_gain.reshape(1, -1),
        expert_ids[0].T,
        route_weight[0].T,
        store_states,
        k_heads[0],
        q_heads[0],
        values[0],
        w_gate[0],
        w_up[0],
        w_down[0],
    )
    return (out[None], store_out)


def solution(mesh):
    return jax.shard_map(
        shards,
        mesh=mesh,
        in_specs=(
            P("expert", "segment", None),
            P("expert", "segment", None),
            P("expert", "segment", None),
            P("expert", "segment", None),
            P("expert", "segment", None),
            P(),
            P("expert"),
            P("expert", "segment", None, None),
            P(),
            P("expert"),
            P("expert", "segment", None),
            P("expert", "segment", None),
            P(("segment", "expert"), None, None),
            P(("segment", "expert"), None, None),
            P(("segment", "expert"), None, None),
        ),
        out_specs=(P("expert", "segment", None), P("expert", "segment", None, None)),
        check_vma=False,
    )
```

```python
import jax
import jax.numpy as jnp
from jax import lax
from jax.experimental import pallas as pl
from jax.experimental.pallas import tpu as pltpu
from jax.sharding import PartitionSpec as P

MESH = pl.DeviceIdType.MESH


GROUP = 4
UNROLL = 5
PARTS = 4


def halves(block):
    high = block.astype(jnp.bfloat16)
    low = (block - high.astype(jnp.float32)).astype(jnp.bfloat16)
    return high, low


def left_pair(block):
    high, low = halves(block)
    return jnp.concatenate([high, low], axis=1)


def right_pair(block):
    high, low = halves(block)
    row = jnp.concatenate([high, low], axis=1)
    return jnp.concatenate([row, row], axis=0)


def paired_dot(left, right):
    both = jnp.dot(left, right, preferred_element_type=jnp.float32)
    width = both.shape[1] // 2
    return both[:, :width] + both[:, width:]


def unit_rows(block, factor):
    squares = jnp.sum(block * block, axis=-1, keepdims=True)
    return block * (lax.rsqrt(squares + 1e-06) * factor)


def mixer_kernel(
    len_ref,
    row_ref,
    slot_ref,
    beta_ref,
    decay_ref,
    gain_ref,
    ids_ref,
    weight_ref,
    store_in,
    k_in,
    q_in,
    v_in,
    gate_in,
    up_in,
    down_in,
    out_ref,
    store_out_ref,
    store_ref,
    k_ref,
    q_ref,
    v_ref,
    gate_ref,
    up_ref,
    down_ref,
    routes_ref,
    routes_all,
    index_ref,
    idx_ref,
    mix_ref,
    mixed_ref,
    rows_ref,
    final_ref,
    offer,
    taken,
    origin,
    held,
    passed,
    step_right,
    step_read,
    step_add,
    strength_ref,
    total_ref,
    across_ref,
    climb,
    sink,
    distant,
    pick,
    stage,
    arrive,
    back,
    flat,
    sum_up,
    sum_down,
    got_up,
    got_down,
    tall,
    wide,
    load_sem,
    routes_send,
    routes_recv,
    index_sem,
    offer_send,
    taken_recv,
    origin_send,
    held_recv,
    passed_send,
    ends_send,
    final_recv,
    distant_send,
    distant_recv,
    climb_send,
    climb_recv,
    sink_send,
    sink_recv,
    stage_send,
    arrive_recv,
    back_send,
    back_recv,
    up_send,
    up_recv,
    down_send,
    down_recv,
):
    segments = lax.axis_size("segment")
    columns = lax.axis_size("expert")
    seg = lax.axis_index("segment")
    col = lax.axis_index("expert")
    pairs = segments // 2
    tok = q_ref.shape[0]
    half = tok // 2
    dim = store_ref.shape[-1]
    cached = store_ref.shape[0]
    heads = segments
    share = v_ref.shape[1] // q_ref.shape[1]
    top = ids_ref.shape[0]
    above = lax.rem(seg + 1, segments)
    below = lax.rem(seg + segments - 1, segments)

    def load(source, target, k):
        return pltpu.make_async_copy(source, target, load_sem.at[k])

    for k, (source, target) in enumerate(
        (
            (store_in, store_ref),
            (k_in, k_ref),
            (q_in, q_ref),
            (v_in, v_ref),
            (gate_in, gate_ref),
            (up_in, up_ref),
            (down_in, down_ref),
        )
    ):
        load(source, target, k).start()
    routes_ref[:top] = ids_ref[...].astype(jnp.float32)
    routes_ref[top:] = weight_ref[...]

    barrier = pltpu.get_barrier_semaphore()

    def greet_row(step, carry):
        other = lax.rem(col + step, columns)
        pl.semaphore_signal(barrier, inc=1, device_id=(seg, other), device_id_type=MESH)
        return carry

    def greet_line(step, carry):
        other = lax.rem(seg + step, segments)
        pl.semaphore_signal(barrier, inc=1, device_id=(other, col), device_id_type=MESH)
        return carry

    lax.fori_loop(1, columns, greet_row, 0)
    lax.fori_loop(1, segments, greet_line, 0)
    pl.semaphore_wait(barrier, columns + segments - 2)

    far = segments // 2
    pltpu.make_async_copy(routes_ref, routes_all.at[0], routes_recv).start()

    def routes_copy(step, slot):
        return pltpu.make_async_remote_copy(
            src_ref=routes_ref,
            dst_ref=routes_all.at[slot],
            send_sem=routes_send.at[slot],
            recv_sem=routes_recv,
            device_id=(lax.rem(seg + step, segments), col),
            device_id_type=MESH,
        )

    def routes_out(k, carry):
        routes_copy(k, 2 * k - 1).start()
        routes_copy(segments - k, 2 * k).start()
        return carry

    lax.fori_loop(1, far, routes_out, 0)
    routes_copy(far, segments - 1).start()

    @pl.when(seg == 0)
    def _():
        held[:, :, dim:] = jnp.zeros((heads, dim, dim), jnp.bfloat16)

    load(store_in, store_ref, 0).wait()

    def propose(i, carry):
        other = lax.rem(col + i, columns)
        wanted = row_ref[other]
        block = jnp.zeros((dim, dim), jnp.bfloat16)
        for r in range(cached):
            match = jnp.where(wanted == col * cached + r, 1.0, 0.0)
            match = jnp.full((dim, dim), match, jnp.float32).astype(jnp.bfloat16)
            block = block + store_ref[r, 0] * match
        offer[other] = block

        @pl.when(i == 0)
        def _():
            pltpu.make_async_copy(offer.at[col], taken.at[col], taken_recv).start()

        @pl.when(i > 0)
        def _():
            pltpu.make_async_remote_copy(
                src_ref=offer.at[other],
                dst_ref=taken.at[col],
                send_sem=offer_send,
                recv_sem=taken_recv,
                device_id=(seg, other),
                device_id_type=MESH,
            ).start()

        return carry

    lax.fori_loop(0, columns, propose, 0)

    line = lax.broadcasted_iota(jnp.int32, (tok, tok), 0)
    lane = lax.broadcasted_iota(jnp.int32, (tok, tok), 1)
    place = lax.broadcasted_iota(jnp.int32, (tok, 1), 0)
    valid = jnp.where(place + seg * tok < len_ref[0], 1.0, 0.0)
    along = lax.broadcasted_iota(jnp.int32, (1, tok), 1)
    valid_along = jnp.where(along + seg * tok < len_ref[0], 1.0, 0.0)
    logs = (decay_ref[...].astype(jnp.float32) * valid_along).astype(jnp.bfloat16)
    writes = (beta_ref[...].astype(jnp.float32) * valid_along).astype(jnp.bfloat16)
    lower = jnp.where(line >= lane, 1.0, 0.0).astype(jnp.bfloat16)
    upper = jnp.where(line <= lane, 1.0, 0.0).astype(jnp.bfloat16)
    diagonal = jnp.where(line == lane, 1.0, 0.0).astype(jnp.bfloat16)
    turned = (((1,), (1,)), ((), ()))
    across_ref[...] = jnp.dot(logs, upper, preferred_element_type=jnp.float32)
    total_ref[...] = lax.dot_general(lower, logs, turned, preferred_element_type=jnp.float32)
    strength_ref[...] = lax.dot_general(
        diagonal, writes, turned, preferred_element_type=jnp.float32
    )
    for k, (source, target) in enumerate(((k_in, k_ref), (q_in, q_ref), (v_in, v_ref))):
        load(source, target, k + 1).wait()
    identity = jnp.where(line == lane, 1.0, 0.0)
    which = lax.broadcasted_iota(jnp.int32, (tok, heads), 1)

    def column_of(ref, j):
        return jnp.sum(jnp.where(which == j, ref[...], 0.0), axis=1, keepdims=True)

    def local_work(i, carry):
        grams, across_keys, unit_keys, unit_queries = [], [], [], []
        for g in range(GROUP):
            spot = pl.ds(pl.multiple_of((i * GROUP + g) * dim, dim), dim)
            keys = unit_rows(k_ref[:, spot].astype(jnp.float32), 1.0)
            queries = unit_rows(q_ref[:, spot].astype(jnp.float32), dim ** (-0.5))
            unit_keys.append(keys)
            unit_queries.append(queries)
            across_keys.append(keys.T)
        for g in range(GROUP):
            grams.append(
                paired_dot(
                    left_pair(jnp.concatenate([unit_keys[g], unit_queries[g]], axis=0)),
                    right_pair(across_keys[g]),
                )
            )
        count = GROUP * share
        number = [i * count + a for a in range(count)]
        strength = [column_of(strength_ref, j) for j in number]
        total = [column_of(total_ref, j) for j in number]
        across = [across_ref[pl.ds(j, 1), :] for j in number]
        upto = [
            jnp.where(line >= lane, jnp.exp(jnp.where(line >= lane, total[a] - across[a], 0.0)), 0.0)
            for a in range(count)
        ]
        coupling = [
            jnp.where(line > lane, strength[a] * upto[a] * grams[a // share][:tok], 0.0)
            for a in range(count)
        ]
        inverse = [
            identity - jnp.where((line == lane + 1) & (line % 2 == 1), coupling[a], 0.0)
            for a in range(count)
        ]
        size = 2
        while size < tok:
            corner = (
                (line // (2 * size) == lane // (2 * size))
                & ((line // size) % 2 == 1)
                & ((lane // size) % 2 == 0)
            )
            inner = [
                paired_dot(
                    left_pair(jnp.where(corner, coupling[a], 0.0)), right_pair(inverse[a])
                )
                for a in range(count)
            ]
            inverse = [
                inverse[a] - paired_dot(left_pair(inverse[a]), right_pair(inner[a]))
                for a in range(count)
            ]
            size *= 2
        growth = [jnp.exp(total[a]) for a in range(count)]
        solver = [left_pair(inverse[a]) for a in range(count)]
        pseudo = []
        for a in range(count):
            spot = pl.ds(pl.multiple_of(number[a] * dim, dim), dim)
            values = v_ref[:, spot].astype(jnp.float32)
            pseudo.append(right_pair(paired_dot(solver[a], right_pair(strength[a] * values))))
        weights = [
            right_pair(
                paired_dot(solver[a], right_pair((strength[a] * growth[a]) * unit_keys[a // share]))
            )
            for a in range(count)
        ]
        for a in range(count):
            last = across[a][:, tok - 1 :]
            tail = across_keys[a // share] * jnp.exp(last - across[a])
            scores = upto[a] * grams[a // share][tok:]
            left = left_pair(jnp.concatenate([tail, scores], axis=0))
            minus = paired_dot(left, weights[a])
            plus = paired_dot(left, pseudo[a])
            step_right[number[a]] = right_pair((jnp.exp(last) * identity - minus[:dim]).T)
            step_add[number[a], :dim] = plus[:dim].T
            step_add[number[a], dim:] = plus[dim:]
            high, low = halves(growth[a] * unit_queries[a // share] - minus[dim:])
            read = jnp.concatenate([high, low], axis=0)
            step_read[number[a]] = jnp.concatenate([read, read], axis=1)
        return carry

    rows_each = dim // PARTS

    def hand_on(j, h):
        some = pl.ds(h * rows_each, rows_each)
        return pltpu.make_async_remote_copy(
            src_ref=passed.at[j, some],
            dst_ref=held.at[j, some],
            send_sem=passed_send.at[j, h],
            recv_sem=held_recv.at[j, h],
            device_id=(seg + 1, col),
            device_id_type=MESH,
        )

    def origin_copy():
        return pltpu.make_async_remote_copy(
            src_ref=origin,
            dst_ref=held.at[seg, :, pl.ds(0, dim)],
            send_sem=origin_send,
            recv_sem=held_recv.at[seg, 0],
            device_id=(0, col),
            device_id_type=MESH,
        )

    def end_copy(j):
        return pltpu.make_async_remote_copy(
            src_ref=passed.at[j],
            dst_ref=final_ref,
            send_sem=ends_send.at[j],
            recv_sem=final_recv,
            device_id=(j, col),
            device_id_type=MESH,
        )

    def give_origin():
        pltpu.make_async_copy(taken, taken, taken_recv).wait()

        def add_up(i, block):
            return block + taken[i].astype(jnp.float32)

        block = lax.fori_loop(0, columns, add_up, jnp.zeros((dim, dim), jnp.float32))
        origin[...] = block.T.astype(jnp.bfloat16)

        @pl.when(seg == 0)
        def _():
            pltpu.make_async_copy(origin, held.at[0, :, pl.ds(0, dim)], held_recv.at[0, 0]).start()

        @pl.when(seg > 0)
        def _():
            origin_copy().start()

    lax.fori_loop(0, heads // share // GROUP, local_work, 0)

    names = lax.broadcasted_iota(jnp.int32, (columns, 1), 0) + seg * columns
    token = lax.broadcasted_iota(jnp.int32, (columns, tok), 1)

    def locate(slot):
        routes = routes_all[slot]
        top = routes.shape[0] // 2
        weight = jnp.zeros((columns, tok), jnp.float32)
        first = jnp.full((columns, tok), tok, jnp.int32)
        last = jnp.full((columns, tok), -1, jnp.int32)
        for k in range(top):
            same = routes[k : k + 1, :].astype(jnp.int32) == names
            weight = weight + jnp.where(same, routes[top + k : top + k + 1, :], 0.0)
            first = jnp.where(same, token, first)
            last = jnp.where(same, token, last)
        first = jnp.min(first, axis=1, keepdims=True)
        last = jnp.max(last, axis=1, keepdims=True)
        index_ref[slot] = jnp.where(token == 0, jnp.where(first < tok, first, 0), jnp.maximum(last, 0))
        pltpu.make_async_copy(index_ref.at[slot], idx_ref.at[slot], index_sem).start()
        at_first = jnp.where(token == first, weight, 0.0)
        at_last = jnp.where((token == last) & (last != first), weight, 0.0)
        return at_first, at_last

    def tabulate(slot, p, source, width):
        at_first, at_last = locate(slot)
        tall[:tok] = jnp.zeros((tok, tok), jnp.float32)
        tall[pl.ds(2 * source, columns, stride=width), :] = at_first
        tall[pl.ds(2 * source + 1, columns, stride=width), :] = at_last
        mix_ref[p, source] = left_pair(tall[:tok].T)

    def chain(j, carry):
        for h in range(PARTS):
            some = pl.ds(h * rows_each, rows_each)
            if h == 0:

                @pl.when(seg == 0)
                def _():
                    piece = held.at[j, :, pl.ds(0, dim)]
                    pltpu.make_async_copy(piece, piece, held_recv.at[j, 0]).wait()

            @pl.when(seg > 0)
            def _():
                piece = held.at[j, some]
                pltpu.make_async_copy(piece, piece, held_recv.at[j, h]).wait()

            passed[j, some] = left_pair(
                paired_dot(held[j, some], step_right[j]) + step_add[j, some]
            )

            @pl.when(seg < segments - 1)
            def _():
                hand_on(j, h).start()

        @pl.when((seg == segments - 1) & (j < segments - 1))
        def _():
            end_copy(j).start()

        @pl.when((seg == segments - 1) & (j == segments - 1))
        def _():
            pltpu.make_async_copy(passed.at[j], final_ref, final_recv).start()

        both = lax.dot_general(
            step_read[j], held[j], turned, preferred_element_type=jnp.float32
        )
        raw = (both[:tok] + both[tok:] + step_add[j, dim:]) * valid
        squares = jnp.sum(raw * raw, axis=-1, keepdims=True) * (1.0 / dim)
        normed = raw * lax.rsqrt(squares + 1e-06) * gain_ref[...]
        mixed_ref[:, pl.ds(pl.multiple_of(j * dim, dim), dim)] = normed.astype(jnp.bfloat16)
        tall[pl.ds(j, tok, stride=heads), :] = normed
        return carry

    def tables(k, carry):
        tabulate(2 * k - 1, k, 0, 4)
        tabulate(2 * k, k, 1, 4)
        return carry

    pltpu.make_async_copy(routes_all, routes_all, routes_recv).wait()
    tabulate(0, 0, 0, 4)
    tabulate(segments - 1, far, 0, 2)
    give_origin()
    lax.fori_loop(1, far, tables, 0)
    lax.fori_loop(0, heads, chain, 0)
    rows_ref[...] = tall[...].astype(jnp.bfloat16).reshape(tok, heads, dim)
    pltpu.make_async_copy(index_ref, idx_ref, index_sem).wait()

    def part(ref, h):
        return ref.at[pl.ds(h * half, half)]

    def climb_copy(source, slot, h):
        return pltpu.make_async_remote_copy(
            src_ref=part(source, h),
            dst_ref=part(climb.at[slot], h),
            send_sem=climb_send.at[slot, h],
            recv_sem=climb_recv.at[slot, h],
            device_id=(above, col),
            device_id_type=MESH,
        )

    def sink_copy(source, slot, h):
        return pltpu.make_async_remote_copy(
            src_ref=part(source, h),
            dst_ref=part(sink.at[slot], h),
            send_sem=sink_send.at[slot, h],
            recv_sem=sink_recv.at[slot, h],
            device_id=(below, col),
            device_id_type=MESH,
        )

    def distant_copy(source, target, h):
        return pltpu.make_async_remote_copy(
            src_ref=part(source, h),
            dst_ref=part(distant, h),
            send_sem=distant_send.at[h],
            recv_sem=distant_recv.at[h],
            device_id=(target, col),
            device_id_type=MESH,
        )

    for h in range(2):
        climb_copy(rows_ref, 1, h).start()
        sink_copy(rows_ref, 1, 1 - h).start()
    climb[0] = rows_ref[...]
    sink[0] = rows_ref[...]
    flat[pairs] = jnp.zeros(flat.shape[1:], jnp.bfloat16)
    got_up[0, pl.ds(half, half)] = jnp.zeros((half, mixed_ref.shape[1]), jnp.bfloat16)
    got_down[0, pl.ds(0, half)] = jnp.zeros((half, mixed_ref.shape[1]), jnp.bfloat16)

    def rows_to_wide(rows, count):
        tall[: count * heads, :] = rows.reshape(count * heads, dim).astype(jnp.float32)
        for j in range(heads):
            wide[:count, j * dim : (j + 1) * dim] = tall[
                pl.ds(j, count, stride=heads), :
            ].astype(jnp.bfloat16)

    def to_all(step):
        def some_of(i, carry):
            for u in range(UNROLL):
                step(1 + i * UNROLL + u)
            return carry

        rounds = (columns - 1) // UNROLL
        lax.fori_loop(0, rounds, some_of, 0)
        for rest in range(1 + rounds * UNROLL, columns):
            step(rest)

    def keep_own(source, target, recv_sem, p, each):
        some = pl.ds(0, each)
        pltpu.make_async_copy(
            source.at[p, col, some], target.at[p, col, some], recv_sem.at[p]
        ).start()

    def send_out(source, target, send_sem, recv_sem, p, other, each):
        some = pl.ds(0, each)
        pltpu.make_async_remote_copy(
            src_ref=source.at[p, other, some],
            dst_ref=target.at[p, col, some],
            send_sem=send_sem.at[p],
            recv_sem=recv_sem.at[p],
            device_id=(seg, other),
            device_id_type=MESH,
        ).start()

    def wait_all(target, sem, p, each):
        piece = target.at[p, :, pl.ds(0, each)]
        pltpu.make_async_copy(piece, piece, sem.at[p]).wait()

    def wait_sent(source, sem, p, each):
        piece = source.at[p, pl.ds(0, columns - 1), pl.ds(0, each)]
        pltpu.make_async_copy(piece, piece, sem.at[p]).wait()

    def dispatch(p, each, slots):
        def choose(other):
            for r in range(each):
                stage[p, other, r] = pick[r // 2, idx_ref[slots[r // 2], other, r % 2]]

        def step(i):
            other = lax.rem(col + i, columns)
            choose(other)
            send_out(stage, arrive, stage_send, arrive_recv, p, other, each)

        to_all(step)
        choose(col)
        keep_own(stage, arrive, arrive_recv, p, each)

    def experts(p, each):
        count = columns * each
        wait_all(arrive, arrive_recv, p, each)
        wait_sent(stage, stage_send, p, each)
        rows_to_wide(arrive[p, :, :each].reshape(count, heads, dim), count)
        rows = wide[:count, :]
        gate_part = jnp.dot(rows, gate_ref[...], preferred_element_type=jnp.float32)
        up_part = jnp.dot(rows, up_ref[...], preferred_element_type=jnp.float32)
        hidden = (gate_part * jax.nn.sigmoid(gate_part) * up_part).astype(jnp.bfloat16)
        for j in range(heads):
            tall[pl.ds(j, count, stride=heads), :] = jnp.dot(
                hidden,
                down_ref[:, j * dim : (j + 1) * dim],
                preferred_element_type=jnp.float32,
            )
        stage[p, :, :each] = (
            tall[: count * heads, :].astype(jnp.bfloat16).reshape(columns, each, heads, dim)
        )

        def step(i):
            send_out(stage, back, back_send, back_recv, p, lax.rem(col + i, columns), each)

        to_all(step)
        keep_own(stage, back, back_recv, p, each)

    def land(p, each):
        count = columns * each
        wait_all(back, back_recv, p, each)
        rows_to_wide(back[p, :, :each].reshape(count, heads, dim), count)
        flat[p, pl.ds(0, count)] = wide[:count, :]

    def gather_step(p, carry):
        for h in range(2):
            @pl.when(p >= 1)
            def _():
                climb_copy(rows_ref, p, h).wait_recv()

            @pl.when((p >= 1) & (p < pairs - 1))
            def _():
                climb_copy(climb.at[p], p + 1, h).start()

            @pl.when(p >= 1)
            def _():
                sink_copy(rows_ref, p, 1 - h).wait_recv()

            @pl.when((p >= 1) & (p < pairs - 1))
            def _():
                sink_copy(sink.at[p], p + 1, 1 - h).start()

            if h == 0:

                @pl.when(p == pairs - 1)
                def _():
                    distant_copy(climb.at[pairs - 1], above, 0).start()
                    distant_copy(sink.at[pairs - 1], below, 1).start()

        pick[0] = climb[p]
        pick[1] = sink[p]
        dispatch(p, 4, (jnp.maximum(2 * p - 1, 0), 2 * p))

        @pl.when(p == 1)
        def _():
            for k, (source, target) in enumerate(
                ((gate_in, gate_ref), (up_in, up_ref), (down_in, down_ref))
            ):
                load(source, target, k + 4).wait()

        @pl.when(p >= 1)
        def _():
            experts(p - 1, 4)

        @pl.when(p >= 2)
        def _():
            land(p - 2, 4)

        return carry

    lax.fori_loop(0, pairs, gather_step, 0)
    for h in range(2):
        distant_copy(rows_ref, above, h).wait_recv()
    pick[0] = distant[...]
    dispatch(pairs, 2, (segments - 1,))
    experts(pairs - 1, 4)
    land(pairs - 2, 4)
    experts(pairs, 2)
    land(pairs - 1, 4)
    land(pairs, 2)

    def term(p, source, h):
        weights = mix_ref[p, source, pl.ds(h * half, half), :]
        rows = flat[p]
        slots = rows.shape[0]
        return jnp.dot(
            weights[:, :slots], rows, preferred_element_type=jnp.float32
        ) + jnp.dot(weights[:, slots:], rows, preferred_element_type=jnp.float32)

    def up_copy(i, h):
        return pltpu.make_async_remote_copy(
            src_ref=part(sum_up.at[lax.rem(i, 2)], h),
            dst_ref=part(got_up.at[i], h),
            send_sem=up_send.at[i, h],
            recv_sem=up_recv.at[i, h],
            device_id=(above, col),
            device_id_type=MESH,
        )

    def down_copy(i, h):
        return pltpu.make_async_remote_copy(
            src_ref=part(sum_down.at[lax.rem(i, 2)], h),
            dst_ref=part(got_down.at[i], h),
            send_sem=down_send.at[i, h],
            recv_sem=down_recv.at[i, h],
            device_id=(below, col),
            device_id_type=MESH,
        )

    sum_up[0, pl.ds(0, half)] = term(pairs, 0, 0).astype(jnp.bfloat16)
    up_copy(0, 0).start()
    sum_down[0, pl.ds(half, half)] = term(pairs, 0, 1).astype(jnp.bfloat16)
    down_copy(0, 1).start()

    def reduce_step(i, carry):
        for h in range(2):
            rise, fall = 1 - h, h
            spot = pl.ds(rise * half, half)
            mine = term(pairs - i, 1, rise)

            @pl.when((i > 1) | (rise == 0))
            def _():
                up_copy(i - 1, rise).wait_recv()

            @pl.when((i > 2) | ((i == 2) & (rise == 0)))
            def _():
                up_copy(i - 2, rise).wait_send()

            sum_up[lax.rem(i, 2), spot] = (mine + got_up[i - 1, spot].astype(jnp.float32)).astype(
                jnp.bfloat16
            )
            up_copy(i, rise).start()
            spot = pl.ds(fall * half, half)
            mine = term(pairs - i, 0, fall)

            @pl.when((i > 1) | (fall == 1))
            def _():
                down_copy(i - 1, fall).wait_recv()

            @pl.when((i > 2) | ((i == 2) & (fall == 1)))
            def _():
                down_copy(i - 2, fall).wait_send()

            sum_down[lax.rem(i, 2), spot] = (
                mine + got_down[i - 1, spot].astype(jnp.float32)
            ).astype(jnp.bfloat16)
            down_copy(i, fall).start()

        return carry

    lax.fori_loop(1, pairs, reduce_step, 0)
    for h in range(2):
        spot = pl.ds(h * half, half)
        total = mixed_ref[spot, :].astype(jnp.float32) + term(0, 0, h)
        up_copy(pairs - 1, h).wait_recv()
        total = total + got_up[pairs - 1, spot].astype(jnp.float32)
        down_copy(pairs - 1, h).wait_recv()
        total = total + got_down[pairs - 1, spot].astype(jnp.float32)
        out_ref[spot, :] = total.astype(jnp.bfloat16)

    def drain(p, carry):
        wait_sent(stage, back_send, p, 4)
        for h in range(2):

            @pl.when(p >= 1)
            def _():
                climb_copy(rows_ref, p, h).wait_send()
                sink_copy(rows_ref, p, h).wait_send()

            @pl.when(p >= pairs - 2)
            def _():
                up_copy(p, h).wait_send()
                down_copy(p, h).wait_send()

        return carry

    lax.fori_loop(0, pairs, drain, 0)
    wait_sent(stage, back_send, pairs, 2)
    for h in range(2):
        distant_copy(rows_ref, above, h).wait_send()
    pltpu.make_async_copy(final_ref, final_ref, final_recv).wait()

    checkpoint = final_ref[:, :dim].astype(jnp.float32).T
    for r in range(cached):
        replaced = jnp.where(slot_ref[0] == r, 1.0, 0.0)
        store_out_ref[r, 0] = (
            checkpoint * replaced
            + store_ref[r, 0].astype(jnp.float32) * (1.0 - replaced)
        ).astype(jnp.bfloat16)

    def routes_sent(k, carry):
        routes_copy(k, 2 * k - 1).wait_send()
        routes_copy(segments - k, 2 * k).wait_send()
        return carry

    lax.fori_loop(1, far, routes_sent, 0)
    routes_copy(far, segments - 1).wait_send()
    sent = offer.at[pl.ds(0, columns - 1)]
    pltpu.make_async_copy(sent, sent, offer_send).wait()

    @pl.when(seg > 0)
    def _():
        origin_copy().wait_send()

    def drain(j, carry):
        @pl.when(seg < segments - 1)
        def _():
            for h in range(PARTS):
                hand_on(j, h).wait_send()

        @pl.when((seg == segments - 1) & (j < segments - 1))
        def _():
            end_copy(j).wait_send()

        return carry

    lax.fori_loop(0, heads, drain, 0)


def mixer(lengths, places, slots, beta, decay, gain, ids, weights, store, k, q, v, w_gate, w_up, w_down):
    segments = lax.axis_size("segment")
    columns = lax.axis_size("expert")
    pairs = segments // 2
    heads = segments
    tok, width = v.shape
    dim = store.shape[-1]
    top = ids.shape[0]
    bf, f32 = jnp.bfloat16, jnp.float32
    dma = pltpu.SemaphoreType.DMA
    whole = pl.BlockSpec(memory_space=pltpu.VMEM)
    scalars = pl.BlockSpec(memory_space=pltpu.SMEM)
    remote = pl.BlockSpec(memory_space=pl.ANY)
    return pl.pallas_call(
        mixer_kernel,
        out_shape=(
            jax.ShapeDtypeStruct((tok, width), bf),
            jax.ShapeDtypeStruct(store.shape, bf),
        ),
        in_specs=[scalars] * 3 + [whole] * 5 + [remote] * 7,
        out_specs=(whole, whole),
        scratch_shapes=[
            pltpu.VMEM(store.shape, bf),
            pltpu.VMEM(k.shape, bf),
            pltpu.VMEM(q.shape, bf),
            pltpu.VMEM(v.shape, bf),
            pltpu.VMEM(w_gate.shape, bf),
            pltpu.VMEM(w_up.shape, bf),
            pltpu.VMEM(w_down.shape, bf),
            pltpu.VMEM((2 * top, tok), f32),
            pltpu.VMEM((segments, 2 * top, tok), f32),
            pltpu.VMEM((segments, columns, tok), jnp.int32),
            pltpu.SMEM((segments, columns, tok), jnp.int32),
            pltpu.VMEM((pairs + 1, 2, tok, 2 * tok), bf),
            pltpu.VMEM((tok, width), bf),
            pltpu.VMEM((tok, heads, dim), bf),
            pltpu.VMEM((dim, 2 * dim), bf),
            pltpu.VMEM((columns, dim, dim), bf),
            pltpu.VMEM((columns, dim, dim), bf),
            pltpu.VMEM((dim, dim), bf),
            pltpu.VMEM((heads, dim, 2 * dim), bf),
            pltpu.VMEM((heads, dim, 2 * dim), bf),
            pltpu.VMEM((heads, 2 * dim, 2 * dim), bf),
            pltpu.VMEM((heads, 2 * dim, 2 * dim), bf),
            pltpu.VMEM((heads, 2 * dim, dim), f32),
            pltpu.VMEM((tok, heads), f32),
            pltpu.VMEM((tok, heads), f32),
            pltpu.VMEM((heads, tok), f32),
            pltpu.VMEM((pairs, tok, heads, dim), bf),
            pltpu.VMEM((pairs, tok, heads, dim), bf),
            pltpu.VMEM((tok, heads, dim), bf),
            pltpu.VMEM((2, tok, heads, dim), bf),
            pltpu.VMEM((pairs + 1, columns, 4, heads, dim), bf),
            pltpu.VMEM((pairs + 1, columns, 4, heads, dim), bf),
            pltpu.VMEM((pairs + 1, columns, 4, heads, dim), bf),
            pltpu.VMEM((pairs + 1, columns * 4, width), bf),
            pltpu.VMEM((2, tok, width), bf),
            pltpu.VMEM((2, tok, width), bf),
            pltpu.VMEM((pairs, tok, width), bf),
            pltpu.VMEM((pairs, tok, width), bf),
            pltpu.VMEM((tok * heads, dim), f32),
            pltpu.VMEM((tok, width), bf),
            dma((7,)),
            dma((segments,)),
            dma,
            dma,
            dma,
            dma,
            dma,
            dma((heads, PARTS)),
            dma((heads, PARTS)),
            dma((heads,)),
            dma,
            dma((2,)),
            dma((2,)),
            dma((pairs, 2)),
            dma((pairs, 2)),
            dma((pairs, 2)),
            dma((pairs, 2)),
            dma((pairs + 1,)),
            dma((pairs + 1,)),
            dma((pairs + 1,)),
            dma((pairs + 1,)),
            dma((pairs, 2)),
            dma((pairs, 2)),
            dma((pairs, 2)),
            dma((pairs, 2)),
        ],
        compiler_params=pltpu.CompilerParams(
            collective_id=1, has_side_effects=True, vmem_limit_bytes=62 * 1024 * 1024
        ),
    )(lengths, places, slots, beta, decay, gain, ids, weights, store, k, q, v, w_gate, w_up, w_down)


def shards(
    q_heads,
    k_heads,
    values,
    beta,
    decay,
    head_gain,
    suffix_len,
    store_states,
    cache_row,
    write_slot,
    expert_ids,
    route_weight,
    w_gate,
    w_up,
    w_down,
):
    out, store_out = mixer(
        suffix_len,
        cache_row,
        write_slot,
        beta[0].T,
        decay[0].T,
        head_gain.reshape(1, -1),
        expert_ids[0].T,
        route_weight[0].T,
        store_states,
        k_heads[0],
        q_heads[0],
        values[0],
        w_gate[0],
        w_up[0],
        w_down[0],
    )
    return (out[None], store_out)


def solution(mesh):
    return jax.shard_map(
        shards,
        mesh=mesh,
        in_specs=(
            P("expert", "segment", None),
            P("expert", "segment", None),
            P("expert", "segment", None),
            P("expert", "segment", None),
            P("expert", "segment", None),
            P(),
            P("expert"),
            P("expert", "segment", None, None),
            P(),
            P("expert"),
            P("expert", "segment", None),
            P("expert", "segment", None),
            P(("segment", "expert"), None, None),
            P(("segment", "expert"), None, None),
            P(("segment", "expert"), None, None),
        ),
        out_specs=(P("expert", "segment", None), P("expert", "segment", None, None)),
        check_vma=False,
    )
```
